32 devices in a mesh: groups: 2 (over y), fsdp: 4 (over x, core), tp: 4 (over z).
Axes of the slice: x: 2, y: 2, z: 4, core: 2. Of those that a mesh axis runs over, the one named last changes fastest.
Arguments:
- hidden_in: bfloat16 [8192, 8192], P(('groups', 'fsdp', 'tp')), parts along dimension 0, may hold values from -6 to 6
- segment_ids: int32 [8192], P(('groups', 'fsdp', 'tp')), parts along dimension 0, may hold values from 0 to 15, never falling along the last dimension, each value on 1 to 512 neighbouring positions
- norm_gain: float32 [16384], P('groups'), parts along dimension 0, may hold values from 0.25 to 1.75
- query_weight: bfloat16 [16384, 4096], P(('groups', 'fsdp', 'tp')), parts along dimension 0, may hold values from -3 to 3
- key_weight: bfloat16 [16384, 512], P(('groups', 'fsdp', 'tp')), parts along dimension 0, may hold values from -3 to 3
- value_weight: bfloat16 [16384, 512], P(('groups', 'fsdp', 'tp')), parts along dimension 0, may hold values from -0.0625 to 0.0625
- output_weight: bfloat16 [16384, 4096], P(('groups', 'fsdp', 'tp')), parts along dimension 0, may hold values from -0.09375 to 0.09375
- query_bias: float32 [8192], P('groups'), parts along dimension 0, may hold values from -3 to 3
- key_bias: float32 [1024], P('groups'), parts along dimension 0, may hold values from -3 to 3
- value_bias: float32 [1024], P('groups'), parts along dimension 0, may hold values from -3 to 3
Outputs:
- hidden_out: bfloat16 [8192, 8192], P(('groups', 'fsdp', 'tp')), parts along dimension 0
The draws below stay inside these ranges and needn't reach their ends.
There are 2 independent parts, one for each index of `groups`. The reference program is written for one: setup_inputs(seed, part) draws one part's arguments, and reference() takes and returns one part's arrays. A program takes and returns all parts, laid end to end along the dimension named above; each array names one. Nothing has to cross between parts.
Inputs may be any that keep to these rules, and one draw needn't show every extreme that they name: `segment_ids`: ids never fall along the rows; each id covers 1 to 512 consecutive rows, and some id covers exactly 512.
All inputs are finite; a program needn't handle non-finite values.
Results may differ from the reference program's by a relative error of at most 0.012.
The reference program's roundings to bfloat16 on the way count: a program that leaves them out, or rounds other values in their place, can miss the bound.
Values may be sent and summed in bfloat16 or wider, within the bound.
No kernel may reach another device: no remote copies, remote signals or barrier semaphores. Data moves between devices by JAX's collectives and lax.ppermute only.
A program may use at most 192 MiB of HBM per device.

```python
import math
import jax
import jax.numpy as jnp
import numpy as np
from jax import lax

D = 8192
QH = 32
KVH = 4
HEAD = 128
TOK = 1024
QW = 4096
KW = 512
ROWS = 4096
N_FSDP = 4
N_TP = 4


def shared_base(key):
    base_key = jax.random.fold_in(key, 11)
    return jax.random.truncated_normal(base_key, -4.0, 4.0, (D, QH * HEAD), jnp.float32) * D ** (-0.5)


def draw_query_weight(key, part):
    base = shared_base(key)
    return base.astype(jnp.bfloat16)


def draw_key_weight(key, part):
    key = jax.random.fold_in(key, 2)
    own_part = jax.random.truncated_normal(key, -4.0, 4.0, (D, KVH * HEAD), jnp.float32) * D ** (-0.5)
    return own_part.astype(jnp.bfloat16)


def shard_levels(key, dims, cuts, least, largest):
    def one(dim, parts):
        steps = jax.random.uniform(jax.random.fold_in(jax.random.fold_in(key, 6), dim), (parts,), jnp.float32, least / len(cuts), largest / len(cuts))
        return jnp.repeat(jnp.exp(steps), dims[dim] // parts).reshape((-1,) + (1,) * (len(dims) - dim - 1))

    loudness = one(*cuts[0])
    for cut in cuts[1:]:
        loudness = loudness * one(*cut)
    return loudness


def split_up(count, total, bound, lean):
    weights = [(1 << 20) // math.isqrt(rank ** lean) + 1 for rank in range(2, count + 1)]
    spare, counts = total - bound - (count - 1), [1] * (count - 1)
    while spare > 0:
        movable = [i for i in range(count - 1) if counts[i] < bound]
        mass, remaining = sum([weights[i] for i in movable]), spare
        for i in movable:
            addition = min(bound - counts[i], max(1, remaining * weights[i] // mass), spare)
            counts[i] = counts[i] + addition
            spare = spare - addition
    return np.array([bound] + counts)


def ragged(own_key, count, total, limit, lean):
    if count == 2:
        one = jax.random.randint(own_key, (), max(1, total - limit), min(limit, total - 1) + 1)
        return jnp.stack([one, total - one])
    sizes = jnp.asarray(split_up(count, total, limit, lean), jnp.int32)
    couples = (count - 1) // 2
    donor, sink = sizes[1:1 + 2 * couples:2], sizes[2:2 + 2 * couples:2]
    slack = jnp.minimum(donor - 1, limit - sink)
    moved = jax.random.randint(jax.random.fold_in(own_key, 1), (couples,), 0, 1 << 20) % (slack + 1)
    sizes = sizes.at[1:1 + 2 * couples:2].set(donor - moved).at[2:2 + 2 * couples:2].set(sink + moved)
    return sizes[jax.random.permutation(jax.random.fold_in(own_key, 2), count)]


def gaussian(key, dims, scale, most, cuts=(), kind=jnp.bfloat16):
    entries = jax.random.normal(key, dims, jnp.float32) * scale
    if len(cuts) > 0:
        entries = shard_levels(key, dims, cuts, -0.22, 0.18) * entries
    return jnp.clip(entries, min=-most, max=most).astype(kind)


def setup_inputs(seed: int = 0, part: int = 0) -> dict:
    streams_of = jax.random.split(jax.random.key(seed), 11)
    part_splits = jax.random.split(jax.random.fold_in(streams_of[10], part), 11)
    return {
        "hidden_in": gaussian(part_splits[0], (ROWS, D), 1.0, 6.0, ((0, 16),)),
        "segment_ids": jnp.searchsorted(jnp.cumsum(ragged(part_splits[1], 4 * N_FSDP, ROWS, TOK // 2, 1)), jnp.arange(ROWS), side="right").astype(jnp.int32),
        "norm_gain": jnp.clip(1.0 + 0.15 * jax.random.normal(part_splits[2], (D,), jnp.float32), 0.25, 1.75),
        "query_weight": draw_query_weight(jax.random.fold_in(jax.random.fold_in(streams_of[10], part), 71), part),
        "key_weight": draw_key_weight(jax.random.fold_in(jax.random.fold_in(streams_of[10], part), 71), part),
        "value_weight": gaussian(part_splits[5], (D, KW), D ** -0.5, 0.0625, ((0, 16),)),
        "output_weight": gaussian(part_splits[6], (D, QW), QW ** -0.5, 0.09375, ((0, 16),)),
        "query_bias": gaussian(part_splits[7], (QW,), 0.5, 3.0, (), jnp.float32),
        "key_bias": gaussian(part_splits[8], (KW,), 0.5, 3.0, (), jnp.float32),
        "value_bias": gaussian(part_splits[9], (KW,), 0.5, 3.0, (), jnp.float32),
    }


rope_base = 1000000.0
norm_eps = 1e-06

def normalize(hidden, gain):
    widened = hidden.astype(jnp.float32)
    mean_square = lax.optimization_barrier(jnp.mean(widened * widened, axis=-1, keepdims=True))
    return (widened * lax.rsqrt(mean_square + norm_eps) * gain).astype(jnp.bfloat16)

def segment_positions(segments):
    row_count = segments.shape[0]
    places = jnp.arange(row_count, dtype=jnp.int32)
    same_seg = segments[:, None] == segments[None, :]
    starts = lax.optimization_barrier(jnp.min(jnp.where(same_seg, places[None, :], row_count), axis=1))
    return (places - starts).astype(jnp.float32)

def rotary(vectors, positions):
    head_width = vectors.shape[-1]
    half_width = head_width // 2
    frequency = rope_base ** (-(jnp.arange(half_width, dtype=jnp.float32) * 2.0 / head_width))
    angles = positions[:, None] * frequency[None, :]
    cosine = jnp.concatenate([jnp.cos(angles), jnp.cos(angles)], axis=-1)[:, None, :]
    sine_part = jnp.concatenate([jnp.sin(angles), jnp.sin(angles)], axis=-1)[:, None, :]
    turned = jnp.concatenate([-vectors[..., half_width:], vectors[..., :half_width]], axis=-1)
    return vectors * cosine + turned * sine_part

def attend(queries, key_rows, value_rows, segments):
    score_scale = key_rows.shape[-1] ** (-0.5)
    scores = jnp.einsum('tgh,sh->gts', queries.astype(jnp.float32), key_rows.astype(jnp.float32)) * score_scale
    row_ids = jnp.arange(segments.shape[0], dtype=jnp.int32)
    allowed = (row_ids[None, :] <= row_ids[:, None]) & (segments[:, None] == segments[None, :])
    scores = jnp.where(allowed[None], scores, -1e+30)
    row_max = lax.optimization_barrier(jnp.max(scores, axis=-1, keepdims=True))
    weights = jnp.exp(scores - row_max)
    probs = (weights / lax.optimization_barrier(jnp.sum(weights, axis=-1, keepdims=True))).astype(jnp.bfloat16)
    return jnp.einsum('gts,sh->tgh', probs.astype(jnp.float32), value_rows.astype(jnp.float32))

def reference(hidden_in, segment_ids, norm_gain, query_weight, key_weight, value_weight, output_weight, query_bias, key_bias, value_bias):
    normed = normalize(hidden_in, norm_gain)
    group_size = QH // KVH
    block_width = QW // N_TP

    def one_group(inputs):
        tokens, segments, residual = inputs
        positions = segment_positions(segments)
        queries = jnp.dot(tokens, query_weight, preferred_element_type=jnp.float32) + query_bias
        key_rows = jnp.dot(tokens, key_weight, preferred_element_type=jnp.float32) + key_bias
        value_rows = jnp.dot(tokens, value_weight, preferred_element_type=jnp.float32) + value_bias
        queries = rotary(queries.reshape(TOK, QH, HEAD), positions).astype(jnp.bfloat16)
        queries = queries.reshape(TOK, KVH, group_size, HEAD).transpose(1, 0, 2, 3)
        key_rows = rotary(key_rows.reshape(TOK, KVH, HEAD), positions).astype(jnp.bfloat16).transpose(1, 0, 2)
        value_rows = value_rows.astype(jnp.bfloat16).reshape(TOK, KVH, HEAD).transpose(1, 0, 2)

        def per_head(items):
            return attend(items[0], items[1], items[2], segments)
        mixed = lax.map(per_head, (queries, key_rows, value_rows))
        mixed = mixed.transpose(1, 0, 2, 3).reshape(TOK, QW).astype(jnp.bfloat16)

        def add_block(index, running):
            start_col = (index * block_width).astype(jnp.int32)
            heads_part = lax.dynamic_slice_in_dim(mixed, start_col, block_width, 1)
            weight_part = lax.dynamic_slice_in_dim(output_weight, start_col, block_width, 1)
            partial_value = lax.dot_general(heads_part, weight_part, (((1,), (1,)), ((), ())), preferred_element_type=jnp.float32)
            rounded = lax.optimization_barrier(partial_value.astype(jnp.bfloat16))
            return running + rounded.astype(jnp.float32)
        summed = lax.fori_loop(0, N_TP, add_block, jnp.zeros((TOK, D), jnp.float32))
        return (residual.astype(jnp.float32) + summed).astype(jnp.bfloat16)
    outputs = lax.map(one_group, (normed.reshape(N_FSDP, TOK, D), segment_ids.reshape(N_FSDP, TOK), hidden_in.reshape(N_FSDP, TOK, D)))
    return outputs.reshape(ROWS, D)
```

```python
import functools

import jax
import jax.numpy as jnp
from jax import lax
from jax.experimental import pallas as pl
from jax.experimental.pallas import tpu as pltpu
from jax.sharding import PartitionSpec as P

HEAD = 128
LONGEST = 512
rope_base = 1000000.0
norm_eps = 1e-06
MASKED = -1e30
NOWHERE = 1 << 20
LEVEL = ("fsdp", "tp")


LIGHT = pl.CostEstimate(flops=1, bytes_accessed=1, transcendentals=0)
ROOM = pltpu.CompilerParams(vmem_limit_bytes=48 << 20)


def normalize(hidden, gain, order, n_f, depth, cuts):
    rows, width = hidden.shape
    n_t, cut = len(order), depth // cuts
    places = [(k, h, i) for k in range(n_t) for h in range(cuts) for i in range(n_f)]

    def scale(hidden):
        widened = hidden.astype(jnp.float32)
        return lax.rsqrt(jnp.mean(widened * widened, axis=-1, keepdims=True) + norm_eps)

    if cut % 128:
        normed = (hidden.astype(jnp.float32) * scale(hidden) * gain).astype(jnp.bfloat16)
        return jnp.concatenate([
            lax.dynamic_slice_in_dim(normed, (i * n_t + order[k]) * depth + h * cut, cut, 1)
            for k, h, i in places
        ], axis=1)

    def kernel(order_ref, hidden_ref, gain_ref, out_ref):
        factor = scale(hidden_ref[...])
        for place, (k, h, i) in enumerate(places):
            start = pl.multiple_of((i * n_t + order_ref[k]) * depth + h * cut, cut)
            span = pl.ds(start, cut)
            run = hidden_ref[:, span].astype(jnp.float32) * factor * gain_ref[:, span]
            out_ref[:, place * cut:(place + 1) * cut] = run.astype(jnp.bfloat16)

    block = min(64, rows)
    own = pl.BlockSpec((block, width), lambda m, order_ref: (m, 0))
    return pl.pallas_call(
        kernel,
        grid_spec=pltpu.PrefetchScalarGridSpec(
            num_scalar_prefetch=1,
            grid=(rows // block,),
            in_specs=[own, pl.BlockSpec((1, width), lambda m, order_ref: (0, 0))],
            out_specs=own,
        ),
        out_shape=jax.ShapeDtypeStruct(hidden.shape, jnp.bfloat16),
        compiler_params=ROOM,
        cost_estimate=LIGHT,
    )(jnp.stack(order).astype(jnp.int32), hidden, gain[None])


def segment_starts(segments):
    places = jnp.arange(segments.shape[-1], dtype=jnp.int32)
    same = segments[:, None] == segments[None, :]
    return jnp.min(jnp.where(same, places, segments.shape[-1]), axis=-1)


def rotary_tables(positions):
    half = HEAD // 2
    frequency = rope_base ** (-(jnp.arange(half, dtype=jnp.float32) * 2.0 / HEAD))
    angles = positions[:, None] * frequency[None, :]
    cosine, sine = jnp.cos(angles), jnp.sin(angles)
    return jnp.concatenate([cosine, cosine], -1), jnp.concatenate([-sine, sine], -1)


def attention_kernel(heads, scale, q_ref, bias_ref, cos_ref, sin_ref, start_ref, row_ref,
                     col_ref, k_ref, v_ref, out_ref):
    cosine, sine = cos_ref[...], sin_ref[...]
    columns = col_ref[...]
    allowed = (columns >= start_ref[...]) & (columns <= row_ref[...])
    keys, values = k_ref[0], v_ref[0]
    for head in range(heads):
        span = slice(head * HEAD, (head + 1) * HEAD)
        query = q_ref[:, span] + bias_ref[:, span]
        query = query * cosine + pltpu.roll(query, HEAD // 2, 1) * sine
        scores = lax.dot_general(
            query.astype(jnp.bfloat16), keys, (((1,), (1,)), ((), ())),
            preferred_element_type=jnp.float32,
        ) * scale
        scores = jnp.where(allowed, scores, MASKED)
        weights = jnp.exp(scores - jnp.max(scores, axis=-1, keepdims=True))
        probs = (weights / jnp.sum(weights, axis=-1, keepdims=True)).astype(jnp.bfloat16)
        mixed = jnp.dot(probs, values, preferred_element_type=jnp.float32)
        out_ref[:, span] = mixed.astype(jnp.bfloat16)


def attention(part, *, rows, groups, width, f, projected, bias, cosine, sine, starts, row_ids,
              columns, key_value):
    n_keys = key_value.shape[1]
    mine = lambda g, f_ref: (2 * g + part, 0)

    def place(g, f_ref):
        d = g ^ f_ref[0]
        return (d // 2 + (d % 2) * (groups // 2), 0)

    def kernel(f_ref, *refs):
        attention_kernel(width // HEAD, HEAD ** -0.5, *refs)

    return pl.pallas_call(
        kernel,
        grid_spec=pltpu.PrefetchScalarGridSpec(
            num_scalar_prefetch=1,
            grid=(groups,),
            in_specs=[
                pl.BlockSpec((rows, width), mine),
                pl.BlockSpec((1, width), lambda g, f_ref: (0, 0)),
                pl.BlockSpec((rows, HEAD), mine),
                pl.BlockSpec((rows, HEAD), mine),
                pl.BlockSpec((rows, 1), mine),
                pl.BlockSpec((rows, 1), mine),
                pl.BlockSpec((1, n_keys), lambda g, f_ref: (0, 0)),
                pl.BlockSpec((1, n_keys, HEAD), lambda g, f_ref: (g, 0, 0)),
                pl.BlockSpec((1, n_keys, HEAD), lambda g, f_ref: (g, 0, 1)),
            ],
            out_specs=pl.BlockSpec((rows, width), place),
        ),
        out_shape=jax.ShapeDtypeStruct((groups * rows, width), jnp.bfloat16),
        compiler_params=ROOM,
        cost_estimate=LIGHT,
    )(jnp.full((1,), f, jnp.int32), projected, bias, cosine, sine, starts, row_ids, columns,
      key_value, key_value)


def project(tokens, weights, total=None):
    n_rows, width = tokens.shape[0], weights[0].shape[1]
    block, n_w = min(512, n_rows), len(weights)

    def kernel(*refs):
        part, done = None, 0
        for ref in refs[1:1 + n_w]:
            depth = ref.shape[0]
            more = jnp.dot(
                refs[0][:, done:done + depth], ref[...], preferred_element_type=jnp.float32
            )
            part, done = more if part is None else part + more, done + depth
        refs[-1][...] = part if total is None else part + refs[1 + n_w][...]

    sums = pl.BlockSpec((block, width), lambda m: (m, 0))
    return pl.pallas_call(
        kernel,
        grid=(n_rows // block,),
        in_specs=[pl.BlockSpec((block, tokens.shape[1]), lambda m: (m, 0))]
        + [pl.BlockSpec(w.shape, lambda m: (0, 0)) for w in weights]
        + ([] if total is None else [sums]),
        out_specs=sums,
        out_shape=jax.ShapeDtypeStruct((n_rows, width), jnp.float32),
        input_output_aliases={} if total is None else {1 + n_w: 0},
        compiler_params=ROOM,
        cost_estimate=LIGHT,
    )(tokens, *weights, *([] if total is None else [total]))


def times_transposed(left, right):
    return lax.dot_general(
        left, right, (((1,), (1,)), ((), ())), preferred_element_type=jnp.float32
    ).astype(jnp.bfloat16)


def partials_of_one(mixed, first, second, take_first):
    n_rows, depth = mixed.shape
    width = first.shape[0]
    block = n_rows // 2

    def kernel(take_ref, mixed_ref, first_ref, second_ref, kept_ref, given_ref):
        def multiply(weight_ref, out_ref):
            out_ref[...] = times_transposed(mixed_ref[...], weight_ref[...])

        for taken, weight_ref in ((1, first_ref), (0, second_ref)):
            for half, out_ref in enumerate((given_ref, kept_ref)):
                chosen = (take_ref[0] == taken) & (pl.program_id(0) == half)
                pl.when(chosen)(functools.partial(multiply, weight_ref, out_ref))

    whole = lambda m, take_ref: (0, 0)
    return pl.pallas_call(
        kernel,
        grid_spec=pltpu.PrefetchScalarGridSpec(
            num_scalar_prefetch=1,
            grid=(2,),
            in_specs=[
                pl.BlockSpec((block, depth), lambda m, take_ref: (1 - m, 0)),
                pl.BlockSpec((width, depth), whole),
                pl.BlockSpec((width, depth), whole),
            ],
            out_specs=[pl.BlockSpec((block, width), whole)] * 2,
        ),
        out_shape=[jax.ShapeDtypeStruct((block, width), jnp.bfloat16)] * 2,
        compiler_params=ROOM,
        cost_estimate=LIGHT,
    )(jnp.full((1,), take_first, jnp.int32), mixed, first, second)


def partials_of_two(mixed_a, mixed_b, weight):
    n_rows, depth = mixed_a.shape
    width = weight.shape[0]
    block = n_rows // 2

    def kernel(a_ref, b_ref, weight_ref, kept_ref, given_ref):
        step = pl.program_id(0)
        for place, mixed_ref in enumerate((a_ref, b_ref)):
            for half, out_ref in enumerate((given_ref, kept_ref)):
                def multiply(mixed_ref=mixed_ref, out_ref=out_ref):
                    out_ref[0] = times_transposed(mixed_ref[...], weight_ref[...])

                pl.when(step == 2 * half + place)(multiply)

    rows = pl.BlockSpec((block, depth), lambda m: (1 - m // 2, 0))
    return pl.pallas_call(
        kernel,
        grid=(4,),
        in_specs=[rows, rows, pl.BlockSpec((width, depth), lambda m: (0, 0))],
        out_specs=[
            pl.BlockSpec((1, block, width), lambda m: (jnp.maximum(m - 2, 0), 0, 0)),
            pl.BlockSpec((1, block, width), lambda m: (jnp.minimum(m, 1), 0, 0)),
        ],
        out_shape=[jax.ShapeDtypeStruct((2, block, width), jnp.bfloat16)] * 2,
        compiler_params=ROOM,
        cost_estimate=LIGHT,
    )(mixed_a, mixed_b, weight)


def add_up(result, hidden, terms, other, use_terms, level, n_t, cuts, cut, h, first):
    rows = result.shape[0]
    count = terms[-1].shape[1] // cut
    wide = lambda term: term.astype(jnp.float32)
    if cut % 128:
        total = sum(wide(term[:rows]) for term in terms)
        if other is not None:
            total = jnp.where(use_terms, total, wide(other))
        for i in range(count):
            column = ((first + i) * n_t + level) * cuts * cut + h * cut
            before = wide(lax.dynamic_slice_in_dim(hidden, column, cut, 1))
            result = lax.dynamic_update_slice_in_dim(
                result, (before + total[:, i * cut:(i + 1) * cut]).astype(jnp.bfloat16), column, 1)
        return result

    def kernel(at_ref, result_ref, hidden_ref, *refs):
        total = sum(wide(ref[...]) for ref in refs[:len(terms)])
        if other is not None:
            total = jnp.where(at_ref[1] == 1, total, wide(refs[len(terms)][...]))
        refs[-1][...] = (wide(hidden_ref[...]) + total).astype(jnp.bfloat16)

    place = pl.BlockSpec(
        (rows, cut), lambda i, at_ref: (0, ((first + i) * n_t + at_ref[0]) * cuts + h))
    extra = [] if other is None else [other]
    return pl.pallas_call(
        kernel,
        grid_spec=pltpu.PrefetchScalarGridSpec(
            num_scalar_prefetch=1,
            grid=(count,),
            in_specs=[pl.BlockSpec(memory_space=pl.ANY), place]
            + [pl.BlockSpec((rows, cut), lambda i, at_ref: (0, i))] * (len(terms) + len(extra)),
            out_specs=place,
        ),
        out_shape=jax.ShapeDtypeStruct(result.shape, result.dtype),
        input_output_aliases={1: 0},
        compiler_params=ROOM,
        cost_estimate=LIGHT,
    )(jnp.stack([level, use_terms.astype(jnp.int32)]), result, hidden, *terms, *extra)


def per_device(
    hidden_in,
    segment_ids,
    norm_gain,
    query_weight,
    key_weight,
    value_weight,
    output_weight,
    query_bias,
    key_bias,
    value_bias,
):
    n_f, n_t = lax.axis_size("fsdp"), lax.axis_size("tp")
    f, t = lax.axis_index("fsdp"), lax.axis_index("tp")
    rows, width = hidden_in.shape
    depth = query_weight.shape[0]
    q_cols = query_weight.shape[1] // n_f
    kv_heads = key_weight.shape[1] // HEAD
    kv_head = f * kv_heads // n_f
    cuts = max(1, depth // 256)
    cut = depth // cuts
    n_pairs = n_t // 2
    inner = [2 * j + 1 - j % 2 for j in range(n_pairs)]
    outer = [2 * j + j % 2 for j in range(n_pairs)]
    pair = t // 2
    my_inner = 2 * pair + 1 - pair % 2
    my_outer = 2 * pair + pair % 2
    is_inner = t == my_inner
    inward = [(outer[j], inner[j]) for j in range(n_pairs)]
    outward = [(inner[j], outer[j]) for j in range(n_pairs)]
    every = list(range(n_t))
    tie = lax.optimization_barrier

    def shift(s):
        return [(inner[(j + s) % n_pairs], inner[j]) for j in range(n_pairs)]

    def send(value, pairs):
        return lax.ppermute(value, "tp", pairs)

    def swap(value, d, levels):
        return lax.ppermute(value, LEVEL, [
            (i * n_t + z, (i ^ d) * n_t + z) for i in range(n_f) for z in levels
        ])

    order = []
    for s in range(n_pairs):
        p = (pair + s) % n_pairs
        order += [2 * p + 1 - p % 2, 2 * p + p % 2]

    def by_index(pieces):
        bit = 1
        while bit < n_f:
            here = (f & bit) != 0
            pieces = [jnp.where(here, pieces[d ^ bit], pieces[d]) for d in range(n_f)]
            bit *= 2
        return jnp.concatenate(pieces, axis=0)

    def level_exchange(block_for, levels):
        return by_index([block_for(f)] + [
            swap(block_for(f ^ d), d, levels) for d in range(1, n_f)
        ])

    def projection_block(weights, h):
        def block(c):
            head = c * kv_heads // n_f
            span = slice(h * cut, (h + 1) * cut)
            return jnp.concatenate([
                lax.dynamic_slice_in_dim(weights[0][span], c * q_cols, q_cols, 1),
                lax.dynamic_slice_in_dim(weights[1][span], head * HEAD, HEAD, 1),
                lax.dynamic_slice_in_dim(weights[2][span], head * HEAD, HEAD, 1),
            ], axis=1)
        return block

    segments = lax.all_gather(segment_ids, "tp", axis=0, tiled=True)
    segments, hidden, output_weight, weights = tie(
        (segments, hidden_in, output_weight, (query_weight, key_weight, value_weight)))
    my_starts = lax.dynamic_slice_in_dim(segment_starts(segments), t * rows, rows)
    digits = jnp.stack([my_starts // 256, my_starts % 256], axis=1).astype(jnp.bfloat16)
    digits = jnp.pad(digits, ((0, 0), (0, HEAD - 2)))

    mine = normalize(hidden, norm_gain, order, n_f, depth, cuts)
    part = n_f * depth

    def gather(k, theirs, outputs):
        both = jnp.concatenate([mine[:, k * part:(k + 1) * part], theirs], axis=0)
        chunks = outputs.shape[1] // part
        outputs = jnp.concatenate(
            [outputs[:, c * part:(c + 1) * part] for c in range(chunks)], axis=0)
        payload = jnp.where(is_inner, both, outputs)
        if k == 0:
            payload = jnp.concatenate(
                [payload, jnp.concatenate([digits, their_digits], axis=0)], axis=1)
        return lax.all_gather(payload, "fsdp", axis=0, tiled=True)

    def output_rows(gathered, count):
        blocks = gathered[:, :part].reshape(n_f, -1, count, part)
        column = f * q_cols
        blocks = lax.dynamic_slice(
            blocks, (0, column // part, 0, column % part), (n_f, 1, count, q_cols))
        return blocks.reshape(n_f, count, q_cols)

    count = 2 * rows * part // output_weight.shape[1]
    early = max(width // 2, part)

    own = [level_exchange(projection_block(weights, 0), every)]
    head = send(jnp.concatenate([mine[:, :early], digits], axis=1), inward)
    raw = [send(output_weight[:cut], outward)]
    own, head, raw, mine, weights, output_weight = tie(
        (own, head, raw, mine, weights, output_weight))
    their_digits = head[:, early:]

    def source(k):
        runs = cut // count
        run, at = k // runs, (k % runs) * count
        h, level = run // 2, run % 2
        if h >= cuts:
            return jnp.zeros((count, output_weight.shape[1]), output_weight.dtype)
        some = raw[h] if level == 0 else output_weight[h * cut:(h + 1) * cut]
        return some[at:at + count]

    across = [send(own[0], shift(1))] if n_pairs > 1 else []
    own += [level_exchange(projection_block(weights, h), every) for h in range(1, cuts)]
    tail = send(mine[:, early:], inward)
    ahead = max(1, n_t // 2)
    gathered = [gather(k, head[:, k * part:(k + 1) * part], source(k)) for k in range(ahead)]
    own, across, tail, mine, output_weight, raw = tie((own, across, tail, mine, output_weight, raw))
    theirs = jnp.concatenate([head[:, :early], tail], axis=1)

    beyond = []
    projected = None
    for h in range(cuts):
        if n_pairs > 1 and h + 1 < cuts:
            across.append(send(own[h + 1], shift(1)))
        elif n_pairs > 1 and h:
            across.append(send(beyond[0], shift(1)))
        beyond.append(send(own[h], inward))
        if h + 1 < cuts:
            raw.append(send(output_weight[(h + 1) * cut:(h + 2) * cut], outward))
        if h == 0:
            projected = project(gathered[0], own)
        own, beyond, across, raw, output_weight, projected = tie(
            (own, beyond, across, raw, output_weight, projected))
    gathered += [
        gather(k, theirs[:, k * part:(k + 1) * part], source(k)) for k in range(ahead, n_t)
    ]

    def outer_run(r):
        return jnp.concatenate([
            output_rows(gathered[k], count)
            for k in range(r * (cut // count), (r + 1) * (cut // count))
        ], axis=1).reshape(-1, q_cols)

    at_outer = [outer_run(0)]
    at_inner = [send(at_outer[0], inward)]
    if n_pairs > 1:
        across += [send(w, shift(1)) for w in beyond[len(across) - cuts:]]
    projected = project(gathered[1], beyond, projected)
    if n_pairs > 1:
        projected = project(gathered[2], across[:cuts], projected)
    projected, across, at_inner, at_outer = tie((projected, across, at_inner, at_outer))

    groups = []
    half = n_f // 2
    for s in range(1, n_pairs):
        halves = [(s, r, p) for r in range(2 * cuts) for p in range(2)]
        inside = halves[1:-1]
        groups += [halves[:1]] + [inside[i:i + 2] for i in range(0, len(inside), 2)] + [halves[-1:]]

    def send_group(group):
        return send(jnp.concatenate([
            at_inner[r][p * half * cut:(p + 1) * half * cut] for _, r, p in group
        ], axis=0), shift(group[0][0]))

    arrived = {}

    def arrive(group, got):
        for place, (s, r, p) in enumerate(group):
            arrived[s, r, p] = got[place * half * cut:(place + 1) * half * cut]

    got = send_group(groups[0]) if groups else None
    if len(at_inner) < 2 * cuts:
        at_outer.append(outer_run(1))
        at_inner.append(send(at_outer[1], inward))
    for s in range(1, n_pairs):
        if s > 1:
            across = [send(w, shift(s)) for w in own + beyond]
            projected = project(gathered[2 * s], across[:cuts], projected)
        projected = project(gathered[2 * s + 1], across[cuts:], projected)

    level_ids = jnp.arange(rows, dtype=jnp.int32)
    pair_ids = jnp.concatenate([my_inner * rows + level_ids, my_outer * rows + level_ids])
    row_ids = jnp.tile(pair_ids, n_f)
    digits = gathered[0][:, part:part + 2].astype(jnp.int32)
    starts = digits[:, 0] * 256 + digits[:, 1]
    cosine, sine = rotary_tables((row_ids - starts).astype(jnp.float32))

    key_rows = projected[:, q_cols:q_cols + HEAD]
    key_rows = key_rows + lax.dynamic_slice_in_dim(key_bias, kv_head * HEAD, HEAD)
    turned = jnp.concatenate([key_rows[:, HEAD // 2:], key_rows[:, :HEAD // 2]], axis=-1)
    keys = (key_rows * cosine + turned * sine).astype(jnp.bfloat16)
    values = projected[:, q_cols + HEAD:] + lax.dynamic_slice_in_dim(value_bias, kv_head * HEAD, HEAD)
    values = values.astype(jnp.bfloat16)
    pair_rows = 2 * rows
    key_value = jnp.concatenate(
        [keys.reshape(n_f, pair_rows, HEAD), values.reshape(n_f, pair_rows, HEAD)], axis=-1
    )
    seen, columns = [key_value], [pair_ids]
    for s in range(1, min(n_pairs - 1, -(-(LONGEST - 1) // pair_rows)) + 1):
        seen.append(send(key_value, [(inner[j - s], inner[j]) for j in range(s, n_pairs)]))
        p = pair - s
        ids = jnp.concatenate([
            (2 * p + 1 - p % 2) * rows + level_ids, (2 * p + p % 2) * rows + level_ids
        ])
        columns.append(jnp.where(p >= 0, ids, NOWHERE))
    attend = functools.partial(
        attention, rows=rows, groups=n_f, width=q_cols, f=f, projected=projected,
        bias=lax.dynamic_slice_in_dim(query_bias, f * q_cols, q_cols)[None],
        cosine=cosine, sine=sine, starts=starts[:, None], row_ids=row_ids[:, None],
        columns=jnp.concatenate(columns)[None], key_value=jnp.concatenate(seen, axis=1),
    )
    def between_chips(kept, given):
        crossed = []
        for d in range(2, n_f, 2):
            span = slice(d // 2 * rows, (d // 2 + 1) * rows)
            share = kept[..., span, :].astype(jnp.float32) + given[..., span, :].astype(jnp.float32)
            crossed.append(swap(share.astype(jnp.bfloat16), d, every))
        return crossed

    def own_pair(result, r):
        kept, given = partials_of_one(mixed, at_inner[r], at_outer[r], is_inner)
        given = swap(given, 1, every)
        return [kept, given] + between_chips(kept, given)

    def other_pair(half_run):
        kept, given = partials_of_two(mixed_inner, mixed_outer, arrived[half_run])
        given = swap(given, 1, every)
        crossed = between_chips(kept, given)
        return [kept[:, :rows], given[:, :rows]] + crossed

    def put_own(result, r, terms):
        return add_up(result, hidden_in, terms, None, is_inner, order[r % 2], n_t, cuts, cut, r // 2, 0)

    def put_other(result, half_run, terms):
        s, r, p = half_run
        sums = sum(term[1].astype(jnp.float32) for term in terms).astype(jnp.bfloat16)
        return add_up(
            result, hidden_in, [term[0] for term in terms], send(sums, outward), is_inner,
            order[2 * s + r % 2], n_t, cuts, cut, r // 2, p * half)

    result = hidden_in
    key_value, got, at_inner, at_outer = tie((attend.keywords["key_value"], got, at_inner, at_outer))
    attend.keywords["key_value"] = key_value
    if groups:
        arrive(groups[0], got)
    mixed, waiting = None, list(groups[:1])
    phase = 1
    while phase < max(len(groups), 4):
        got = send_group(groups[phase]) if phase < len(groups) else None
        if len(at_inner) < 2 * cuts:
            at_outer.append(outer_run(len(at_inner)))
            at_inner.append(send(at_outer[-1], inward))
        if phase == 1:
            mixed_outer = attend(1)
            mixed_inner = attend(0)
            mixed_inner, mixed_outer, got, at_inner, at_outer = tie(
                (mixed_inner, mixed_outer, got, at_inner, at_outer))
        else:
            done = {}
            if phase == 2:
                mixed = jnp.where(is_inner, mixed_inner, send(mixed_outer, outward))
            if phase == 3:
                done = {r: own_pair(result, r) for r in range(2 * cuts)}
            else:
                done = {item: other_pair(item) for group in waiting for item in group}
                waiting = []
            done, mixed, got, at_inner, at_outer = tie((done, mixed, got, at_inner, at_outer))
            for item, terms in done.items():
                result = (put_own if phase == 3 else put_other)(result, item, terms)
        if got is not None:
            arrive(groups[phase], got)
            waiting.append(groups[phase])
        phase += 1
    for group in waiting:
        for item in group:
            result = put_other(result, item, other_pair(item))
    return result


def solution(mesh):
    return jax.shard_map(
        per_device,
        mesh=mesh,
        in_specs=(
            P(("groups", "fsdp", "tp"), None),
            P(("groups", "fsdp", "tp")),
            P("groups"),
            P(("groups", "fsdp", "tp"), None),
            P(("groups", "fsdp", "tp"), None),
            P(("groups", "fsdp", "tp"), None),
            P(("groups", "fsdp", "tp"), None),
            P("groups"),
            P("groups"),
            P("groups"),
        ),
        out_specs=P(("groups", "fsdp", "tp"), None),
        check_vma=False,
    )
```

```python
import functools

import jax
import jax.numpy as jnp
from jax import lax
from jax.experimental import pallas as pl
from jax.experimental.pallas import tpu as pltpu
from jax.sharding import PartitionSpec as P

HEAD = 128
LONGEST = 512
rope_base = 1000000.0
norm_eps = 1e-06
MASKED = -1e30
LOG2E = 1.4426950408889634
NOWHERE = 1 << 20
LEVEL = ("fsdp", "tp")


LIGHT = pl.CostEstimate(flops=1, bytes_accessed=1, transcendentals=0)
ROOM = pltpu.CompilerParams(vmem_limit_bytes=48 << 20)


def normalize(hidden, gain, order, n_f, depth, cuts):
    rows, width = hidden.shape
    n_t, cut = len(order), depth // cuts
    places = [(k, h, i) for k in range(n_t) for h in range(cuts) for i in range(n_f)]

    def scale(hidden):
        widened = hidden.astype(jnp.float32)
        return lax.rsqrt(jnp.mean(widened * widened, axis=-1, keepdims=True) + norm_eps)

    if cut % 128:
        normed = (hidden.astype(jnp.float32) * scale(hidden) * gain).astype(jnp.bfloat16)
        return jnp.concatenate([
            lax.dynamic_slice_in_dim(normed, (i * n_t + order[k]) * depth + h * cut, cut, 1)
            for k, h, i in places
        ], axis=1)

    def kernel(order_ref, hidden_ref, gain_ref, out_ref):
        factor = scale(hidden_ref[...])
        for place, (k, h, i) in enumerate(places):
            start = pl.multiple_of((i * n_t + order_ref[k]) * depth + h * cut, cut)
            span = pl.ds(start, cut)
            run = hidden_ref[:, span].astype(jnp.float32) * factor * gain_ref[:, span]
            out_ref[:, place * cut:(place + 1) * cut] = run.astype(jnp.bfloat16)

    block = min(64, rows)
    own = pl.BlockSpec((block, width), lambda m, order_ref: (m, 0))
    return pl.pallas_call(
        kernel,
        grid_spec=pltpu.PrefetchScalarGridSpec(
            num_scalar_prefetch=1,
            grid=(rows // block,),
            in_specs=[own, pl.BlockSpec((1, width), lambda m, order_ref: (0, 0))],
            out_specs=own,
        ),
        out_shape=jax.ShapeDtypeStruct(hidden.shape, jnp.bfloat16),
        compiler_params=ROOM,
        cost_estimate=LIGHT,
    )(jnp.stack(order).astype(jnp.int32), hidden, gain[None])


def segment_starts(segments):
    places = jnp.arange(segments.shape[-1], dtype=jnp.int32)
    same = segments[:, None] == segments[None, :]
    return jnp.min(jnp.where(same, places, segments.shape[-1]), axis=-1)


def rotary_tables(positions):
    half = HEAD // 2
    frequency = rope_base ** (-(jnp.arange(half, dtype=jnp.float32) * 2.0 / HEAD))
    angles = positions[:, None] * frequency[None, :]
    cosine, sine = jnp.cos(angles), jnp.sin(angles)
    return jnp.concatenate([cosine, cosine], -1), jnp.concatenate([-sine, sine], -1)


def attention_kernel(heads, scale, q_ref, bias_ref, cos_ref, sin_ref, start_ref, row_ref,
                     col_ref, k_ref, v_ref, out_ref):
    cosine, sine = cos_ref[...], sin_ref[...]
    columns = col_ref[...]
    allowed = (columns >= start_ref[...]) & (columns <= row_ref[...])
    keys, values = k_ref[0], v_ref[0]
    for head in range(heads):
        span = slice(head * HEAD, (head + 1) * HEAD)
        query = q_ref[:, span] + bias_ref[:, span]
        query = query * cosine + pltpu.roll(query, HEAD // 2, 1) * sine
        scores = lax.dot_general(
            query.astype(jnp.bfloat16), keys, (((1,), (1,)), ((), ())),
            preferred_element_type=jnp.float32,
        )
        scores = jnp.where(allowed, scores, MASKED)
        highest = jnp.max(scores, axis=-1, keepdims=True)
        weights = jnp.exp2((scores - highest) * (scale * LOG2E))
        share = 1.0 / jnp.sum(weights, axis=-1, keepdims=True)
        probs = (weights * share).astype(jnp.bfloat16)
        mixed = jnp.dot(probs, values, preferred_element_type=jnp.float32)
        out_ref[:, span] = mixed.astype(jnp.bfloat16)


def attention(part, *, rows, groups, width, f, projected, bias, cosine, sine, starts, row_ids,
              columns, key_value):
    n_keys = key_value.shape[1]
    mine = lambda g, f_ref: (2 * g + part, 0)

    def place(g, f_ref):
        d = g ^ f_ref[0]
        return (d // 2 + (d % 2) * (groups // 2), 0)

    def kernel(f_ref, *refs):
        attention_kernel(width // HEAD, HEAD ** -0.5, *refs)

    return pl.pallas_call(
        kernel,
        grid_spec=pltpu.PrefetchScalarGridSpec(
            num_scalar_prefetch=1,
            grid=(groups,),
            in_specs=[
                pl.BlockSpec((rows, width), mine),
                pl.BlockSpec((1, width), lambda g, f_ref: (0, 0)),
                pl.BlockSpec((rows, HEAD), mine),
                pl.BlockSpec((rows, HEAD), mine),
                pl.BlockSpec((rows, 1), mine),
                pl.BlockSpec((rows, 1), mine),
                pl.BlockSpec((1, n_keys), lambda g, f_ref: (0, 0)),
                pl.BlockSpec((1, n_keys, HEAD), lambda g, f_ref: (g, 0, 0)),
                pl.BlockSpec((1, n_keys, HEAD), lambda g, f_ref: (g, 0, 1)),
            ],
            out_specs=pl.BlockSpec((rows, width), place),
        ),
        out_shape=jax.ShapeDtypeStruct((groups * rows, width), jnp.bfloat16),
        compiler_params=ROOM,
        cost_estimate=LIGHT,
    )(jnp.full((1,), f, jnp.int32), projected, bias, cosine, sine, starts, row_ids, columns,
      key_value, key_value)


def project(tokens, weights, total=None):
    n_rows, width = tokens.shape[0], weights[0].shape[1]
    block, n_w = min(512, n_rows), len(weights)

    def kernel(*refs):
        part, done = None, 0
        for ref in refs[1:1 + n_w]:
            depth = ref.shape[0]
            more = jnp.dot(
                refs[0][:, done:done + depth], ref[...], preferred_element_type=jnp.float32
            )
            part, done = more if part is None else part + more, done + depth
        refs[-1][...] = part if total is None else part + refs[1 + n_w][...]

    sums = pl.BlockSpec((block, width), lambda m: (m, 0))
    return pl.pallas_call(
        kernel,
        grid=(n_rows // block,),
        in_specs=[pl.BlockSpec((block, tokens.shape[1]), lambda m: (m, 0))]
        + [pl.BlockSpec(w.shape, lambda m: (0, 0)) for w in weights]
        + ([] if total is None else [sums]),
        out_specs=sums,
        out_shape=jax.ShapeDtypeStruct((n_rows, width), jnp.float32),
        input_output_aliases={} if total is None else {1 + n_w: 0},
        compiler_params=ROOM,
        cost_estimate=LIGHT,
    )(tokens, *weights, *([] if total is None else [total]))


def times_transposed(left, right):
    return lax.dot_general(
        left, right, (((1,), (1,)), ((), ())), preferred_element_type=jnp.float32
    ).astype(jnp.bfloat16)


def partials_of_one(mixed, first, second, take_first):
    n_rows, depth = mixed.shape
    width = first.shape[0]
    block = n_rows // 2

    def kernel(take_ref, mixed_ref, first_ref, second_ref, kept_ref, given_ref):
        def multiply(weight_ref, out_ref):
            out_ref[...] = times_transposed(mixed_ref[...], weight_ref[...])

        for taken, weight_ref in ((1, first_ref), (0, second_ref)):
            for half, out_ref in enumerate((given_ref, kept_ref)):
                chosen = (take_ref[0] == taken) & (pl.program_id(0) == half)
                pl.when(chosen)(functools.partial(multiply, weight_ref, out_ref))

    whole = lambda m, take_ref: (0, 0)
    return pl.pallas_call(
        kernel,
        grid_spec=pltpu.PrefetchScalarGridSpec(
            num_scalar_prefetch=1,
            grid=(2,),
            in_specs=[
                pl.BlockSpec((block, depth), lambda m, take_ref: (1 - m, 0)),
                pl.BlockSpec((width, depth), whole),
                pl.BlockSpec((width, depth), whole),
            ],
            out_specs=[pl.BlockSpec((block, width), whole)] * 2,
        ),
        out_shape=[jax.ShapeDtypeStruct((block, width), jnp.bfloat16)] * 2,
        compiler_params=ROOM,
        cost_estimate=LIGHT,
    )(jnp.full((1,), take_first, jnp.int32), mixed, first, second)


def partials_of_two(mixed_a, mixed_b, weight):
    n_rows, depth = mixed_a.shape
    width = weight.shape[0]
    block = n_rows // 2

    def kernel(a_ref, b_ref, weight_ref, kept_ref, given_ref):
        step = pl.program_id(0)
        for place, mixed_ref in enumerate((a_ref, b_ref)):
            for half, out_ref in enumerate((given_ref, kept_ref)):
                def multiply(mixed_ref=mixed_ref, out_ref=out_ref):
                    out_ref[...] = times_transposed(mixed_ref[...], weight_ref[...])

                pl.when(step == 2 * half + place)(multiply)

    rows = pl.BlockSpec((block, depth), lambda m: (1 - m // 2, 0))
    return pl.pallas_call(
        kernel,
        grid=(4,),
        in_specs=[rows, rows, pl.BlockSpec((width, depth), lambda m: (0, 0))],
        out_specs=[
            pl.BlockSpec((block, width), lambda m: (0, jnp.maximum(m - 2, 0))),
            pl.BlockSpec((block, width), lambda m: (0, jnp.minimum(m, 1))),
        ],
        out_shape=[jax.ShapeDtypeStruct((block, 2 * width), jnp.bfloat16)] * 2,
        compiler_params=ROOM,
        cost_estimate=LIGHT,
    )(mixed_a, mixed_b, weight)


def add_up(result, hidden, terms, item, other, other_item, use_terms, count, level, n_t, cuts, cut, h, first):
    rows = result.shape[0]
    wide = lambda term: term.astype(jnp.float32)
    if cut % 128:
        total = sum(wide(term[item, :rows, :count * cut]) for term in terms)
        if other is not None:
            total = jnp.where(use_terms, total, wide(other[other_item]))
        for i in range(count):
            column = ((first + i) * n_t + level) * cuts * cut + h * cut
            before = wide(lax.dynamic_slice_in_dim(hidden, column, cut, 1))
            result = lax.dynamic_update_slice_in_dim(
                result, (before + total[:, i * cut:(i + 1) * cut]).astype(jnp.bfloat16), column, 1)
        return result

    def kernel(at_ref, result_ref, hidden_ref, *refs):
        total = sum(wide(ref[...]) for ref in refs[:len(terms)])
        if other is not None:
            total = jnp.where(at_ref[1] == 1, total, wide(refs[len(terms)][...]))
        refs[-1][...] = (wide(hidden_ref[...]) + total).astype(jnp.bfloat16)

    place = pl.BlockSpec(
        (rows, cut), lambda i, at_ref: (0, ((first + i) * n_t + at_ref[0]) * cuts + h))
    one = lambda item: pl.BlockSpec((None, rows, cut), lambda i, at_ref: (item, 0, i))
    extra = [] if other is None else [other]
    return pl.pallas_call(
        kernel,
        grid_spec=pltpu.PrefetchScalarGridSpec(
            num_scalar_prefetch=1,
            grid=(count,),
            in_specs=[pl.BlockSpec(memory_space=pl.ANY), place]
            + [one(item)] * len(terms) + [one(other_item)] * len(extra),
            out_specs=place,
        ),
        out_shape=jax.ShapeDtypeStruct(result.shape, result.dtype),
        input_output_aliases={1: 0},
        compiler_params=ROOM,
        cost_estimate=LIGHT,
    )(jnp.stack([level, use_terms.astype(jnp.int32)]), result, hidden, *terms, *extra)


def per_device(
    hidden_in,
    segment_ids,
    norm_gain,
    query_weight,
    key_weight,
    value_weight,
    output_weight,
    query_bias,
    key_bias,
    value_bias,
):
    n_f, n_t = lax.axis_size("fsdp"), lax.axis_size("tp")
    f, t = lax.axis_index("fsdp"), lax.axis_index("tp")
    rows, width = hidden_in.shape
    depth = query_weight.shape[0]
    q_cols = query_weight.shape[1] // n_f
    kv_heads = key_weight.shape[1] // HEAD
    kv_head = f * kv_heads // n_f
    cuts = max(1, depth // 256)
    cut = depth // cuts
    n_pairs = n_t // 2
    inner = [2 * j + 1 - j % 2 for j in range(n_pairs)]
    outer = [2 * j + j % 2 for j in range(n_pairs)]
    pair = t // 2
    my_inner = 2 * pair + 1 - pair % 2
    my_outer = 2 * pair + pair % 2
    is_inner = t == my_inner
    inward = [(outer[j], inner[j]) for j in range(n_pairs)]
    outward = [(inner[j], outer[j]) for j in range(n_pairs)]
    every = list(range(n_t))
    tie = lax.optimization_barrier

    def shift(s):
        return [(inner[(j + s) % n_pairs], inner[j]) for j in range(n_pairs)]

    def send(value, pairs):
        return lax.ppermute(value, "tp", pairs)

    def swap(value, d, levels):
        return lax.ppermute(value, LEVEL, [
            (i * n_t + z, (i ^ d) * n_t + z) for i in range(n_f) for z in levels
        ])

    order = []
    for s in range(n_pairs):
        p = (pair + s) % n_pairs
        order += [2 * p + 1 - p % 2, 2 * p + p % 2]

    def by_index(pieces):
        bit = 1
        while bit < n_f:
            here = (f & bit) != 0
            pieces = [jnp.where(here, pieces[d ^ bit], pieces[d]) for d in range(n_f)]
            bit *= 2
        return jnp.concatenate(pieces, axis=0)

    def level_exchange(block_for, levels):
        return by_index([block_for(f)] + [
            swap(block_for(f ^ d), d, levels) for d in range(1, n_f)
        ])

    def projection_block(weights, h):
        def block(c):
            head = c * kv_heads // n_f
            span = slice(h * cut, (h + 1) * cut)
            return jnp.concatenate([
                lax.dynamic_slice_in_dim(weights[0][span], c * q_cols, q_cols, 1),
                lax.dynamic_slice_in_dim(weights[1][span], head * HEAD, HEAD, 1),
                lax.dynamic_slice_in_dim(weights[2][span], head * HEAD, HEAD, 1),
            ], axis=1)
        return block

    segments = lax.all_gather(segment_ids, "tp", axis=0, tiled=True)
    segments, hidden, output_weight, weights = tie(
        (segments, hidden_in, output_weight, (query_weight, key_weight, value_weight)))
    my_starts = lax.dynamic_slice_in_dim(segment_starts(segments), t * rows, rows)
    digits = jnp.stack([my_starts // 256, my_starts % 256], axis=1).astype(jnp.bfloat16)
    digits = jnp.pad(digits, ((0, 0), (0, HEAD - 2)))

    mine = normalize(hidden, norm_gain, order, n_f, depth, cuts)
    part = n_f * depth

    def gather(k, theirs, outputs):
        both = jnp.concatenate([mine[:, k * part:(k + 1) * part], theirs], axis=0)
        chunks = outputs.shape[1] // part
        outputs = jnp.concatenate(
            [outputs[:, c * part:(c + 1) * part] for c in range(chunks)], axis=0)
        payload = jnp.where(is_inner, both, outputs)
        if k == 0:
            payload = jnp.concatenate(
                [payload, jnp.concatenate([digits, their_digits], axis=0)], axis=1)
        return lax.all_gather(payload, "fsdp", axis=0, tiled=True)

    def output_rows(gathered, count):
        blocks = gathered.reshape(n_f, -1, count, gathered.shape[1])
        column = f * q_cols
        blocks = lax.dynamic_slice(
            blocks, (0, column // part, 0, column % part), (n_f, 1, count, q_cols))
        return blocks.reshape(n_f, count, q_cols)

    count = 2 * rows * part // output_weight.shape[1]
    early = max(width * 3 // 8, part)

    own = [level_exchange(projection_block(weights, 0), every)]
    head = send(jnp.concatenate([mine[:, :early], digits], axis=1), inward)
    own, head, mine, weights, output_weight = tie((own, head, mine, weights, output_weight))
    their_digits = head[:, early:]
    raw = []

    def source(k):
        runs = cut // count
        run, at = k // runs, (k % runs) * count
        if run >= 2 * cuts:
            return jnp.zeros((count, output_weight.shape[1]), output_weight.dtype)
        some = raw[run - cuts] if run >= cuts else output_weight[run * cut:(run + 1) * cut]
        return some[at:at + count]

    across = [send(own[0], shift(1))] if n_pairs > 1 else []
    own += [level_exchange(projection_block(weights, h), every) for h in range(1, cuts)]
    tail = send(mine[:, early:], inward)
    gathered = [gather(0, head[:, :part], source(0))]
    own, across, tail, mine, output_weight = tie((own, across, tail, mine, output_weight))
    theirs = jnp.concatenate([head[:, :early], tail], axis=1)

    beyond = []
    projected = None
    for h in range(cuts):
        until = min(n_t, (cuts + h) * (cut // count))
        gathered += [
            gather(k, theirs[:, k * part:(k + 1) * part], source(k))
            for k in range(len(gathered), until)
        ]
        if n_pairs > 1 and h + 1 < cuts:
            across.append(send(own[h + 1], shift(1)))
        elif n_pairs > 1 and h:
            across.append(send(beyond[0], shift(1)))
        beyond.append(send(own[h], inward))
        raw.append(send(output_weight[h * cut:(h + 1) * cut], outward))
        if h == 0:
            projected = project(gathered[0], own)
        own, beyond, across, raw, output_weight, projected, theirs, mine = tie(
            (own, beyond, across, raw, output_weight, projected, theirs, mine))
    gathered += [
        gather(k, theirs[:, k * part:(k + 1) * part], source(k)) for k in range(len(gathered), n_t)
    ]

    def outer_run(r):
        return jnp.concatenate([
            output_rows(gathered[k], count)
            for k in range(r * (cut // count), (r + 1) * (cut // count))
        ], axis=1).reshape(-1, q_cols)

    at_outer = [outer_run(0)]
    at_inner = [send(at_outer[0], inward)]
    if n_pairs > 1:
        across += [send(w, shift(1)) for w in beyond[len(across) - cuts:]]
    projected = project(gathered[1], beyond, projected)
    if n_pairs > 1:
        projected = project(gathered[2], across[:cuts], projected)
    projected, across, at_inner, at_outer = tie((projected, across, at_inner, at_outer))

    groups = []
    half = n_f // 2
    for s in range(1, n_pairs):
        halves = [(s, r, p) for r in range(2 * cuts) for p in range(2)]
        inside = halves[1:-1]
        groups += [halves[:1]] + [inside[i:i + 2] for i in range(0, len(inside), 2)] + [halves[-1:]]

    def send_group(group):
        return send(jnp.concatenate([
            at_inner[r][p * half * cut:(p + 1) * half * cut] for _, r, p in group
        ], axis=0), shift(group[0][0]))

    arrived = {}

    def arrive(group, got):
        for place, (s, r, p) in enumerate(group):
            arrived[s, r, p] = got[place * half * cut:(place + 1) * half * cut]

    got = send_group(groups[0]) if groups else None
    if len(at_inner) < 2 * cuts:
        at_outer.append(outer_run(1))
        at_inner.append(send(at_outer[1], inward))
    for s in range(1, n_pairs):
        if s > 1:
            across = [send(w, shift(s)) for w in own + beyond]
            projected = project(gathered[2 * s], across[:cuts], projected)
        projected = project(gathered[2 * s + 1], across[cuts:], projected)

    level_ids = jnp.arange(rows, dtype=jnp.int32)
    pair_ids = jnp.concatenate([my_inner * rows + level_ids, my_outer * rows + level_ids])
    row_ids = jnp.tile(pair_ids, n_f)
    digits = gathered[0][:, part:part + 2].astype(jnp.int32)
    starts = digits[:, 0] * 256 + digits[:, 1]
    cosine, sine = rotary_tables((row_ids - starts).astype(jnp.float32))

    key_rows = projected[:, q_cols:q_cols + HEAD]
    key_rows = key_rows + lax.dynamic_slice_in_dim(key_bias, kv_head * HEAD, HEAD)
    turned = jnp.concatenate([key_rows[:, HEAD // 2:], key_rows[:, :HEAD // 2]], axis=-1)
    keys = (key_rows * cosine + turned * sine).astype(jnp.bfloat16)
    values = projected[:, q_cols + HEAD:] + lax.dynamic_slice_in_dim(value_bias, kv_head * HEAD, HEAD)
    values = values.astype(jnp.bfloat16)
    pair_rows = 2 * rows
    key_value = jnp.concatenate(
        [keys.reshape(n_f, pair_rows, HEAD), values.reshape(n_f, pair_rows, HEAD)], axis=-1
    )
    seen = [key_value]
    reach = min(n_t - 1, -(-(LONGEST - 1) // rows))
    for s in range(1, min(n_pairs - 1, (reach + 1) // 2) + 1):
        seen.append(send(key_value, [(inner[j - s], inner[j]) for j in range(s, n_pairs)]))

    def attend(outer_rows):
        blocks, columns = [], []
        for d in range(reach + 1):
            found = []
            for parity in range(2):
                offset = (1 - parity) ^ outer_rows
                s = -((offset - d) // 2)
                place = ((offset - d) % 2) ^ (1 - (parity + s) % 2)
                block = seen[s] if s < len(seen) else jnp.zeros_like(key_value)
                found.append(block[:, place * rows:(place + 1) * rows])
            blocks.append(jnp.where(pair % 2 == 0, found[0], found[1]))
            level = (my_outer if outer_rows else my_inner) - d
            columns.append(jnp.where(level >= 0, level * rows + level_ids, NOWHERE))
        return attention(
            outer_rows, rows=rows, groups=n_f, width=q_cols, f=f, projected=projected,
            bias=lax.dynamic_slice_in_dim(query_bias, f * q_cols, q_cols)[None],
            cosine=cosine, sine=sine, starts=starts[:, None], row_ids=row_ids[:, None],
            columns=jnp.concatenate(columns)[None], key_value=jnp.concatenate(blocks, axis=1),
        )

    wide = lambda value: value.astype(jnp.float32)

    def multiply(item):
        if item[0] == 0:
            return partials_of_one(mixed, at_inner[item[1]], at_outer[item[1]], is_inner)
        return partials_of_two(mixed_inner, mixed_outer, arrived[item])

    def between_cores(items, long_ones):
        kept, given = zip(*[multiply(item) for item in items])
        given = tie((jnp.stack(given), long_ones))[0]
        return items, jnp.stack(kept), swap(given, 1, every)

    def between_chips(items, kept, given):
        crossed = []
        for d in range(2, n_f, 2):
            span = slice(d // 2 * rows, (d // 2 + 1) * rows)
            share = wide(kept[:, span]) + wide(given[:, span])
            crossed.append(swap(share.astype(jnp.bfloat16), d, every))
        return items, [kept, given] + crossed

    def between_levels(items, terms):
        others = [i for i, item in enumerate(items) if item[0]]
        if not others:
            return items, terms, None
        sums = [
            sum(wide(term[i, :rows, half * cut:]) for term in terms).astype(jnp.bfloat16)
            for i in others
        ]
        return items, terms, send(jnp.stack(sums), outward)

    def put(result, items, terms, other):
        n_other = 0
        for i, item in enumerate(items):
            level, h = 1 - item[1] // cuts, item[1] % cuts
            if item[0] == 0:
                result = add_up(
                    result, hidden_in, terms, i, None, 0, is_inner, n_f, order[level],
                    n_t, cuts, cut, h, 0)
            else:
                result = add_up(
                    result, hidden_in, terms, i, other, n_other, is_inner, half,
                    order[2 * item[0] + level], n_t, cuts, cut, h, item[2] * half)
                n_other += 1
        return result

    mixed_outer = attend(1)
    mixed_outer, got, at_inner, at_outer, projected, seen = tie(
        (mixed_outer, got, at_inner, at_outer, projected, seen))
    if groups:
        arrive(groups[0], got)
    runs = [(0, r) for r in range(2 * cuts)]
    result, phase, from_cores, from_chips, from_levels = hidden_in, 1, None, None, None
    while phase <= max(len(groups), 3) or from_cores or from_chips or from_levels:
        got = send_group(groups[phase]) if phase < len(groups) else None
        if len(at_inner) < 2 * cuts:
            at_outer.append(outer_run(len(at_inner)))
            at_inner.append(send(at_outer[-1], inward))
        received = from_levels
        from_levels = between_levels(*from_chips) if from_chips else None
        from_chips = between_chips(*from_cores) if from_cores else None
        if phase == 1:
            there = send(mixed_outer, outward)
            mixed_inner = attend(0)
        if phase == 2:
            mixed = jnp.where(is_inner, mixed_inner, there)
        items = list(groups[phase - 1]) if phase <= len(groups) else []
        if phase >= 2:
            ready = runs[:cuts]
            items, runs = items + ready, runs[cuts:]
        long_ones = (got, at_inner[-1:], from_chips and from_chips[1], from_levels and from_levels[2], there)
        from_cores = between_cores(items, long_ones) if items else None
        if received:
            result = put(result, *received)
        moving = [None if x is None else x[1:] for x in (from_cores, from_chips, from_levels)]
        if phase == 1:
            mixed_inner, there = tie((mixed_inner, there))
        moving, got, at_inner, at_outer, result = tie((moving, got, at_inner, at_outer, result))
        from_cores, from_chips, from_levels = [
            None if x is None else (x[0],) + tuple(y)
            for x, y in zip((from_cores, from_chips, from_levels), moving)
        ]
        if got is not None:
            arrive(groups[phase], got)
        phase += 1
    return result


def solution(mesh):
    return jax.shard_map(
        per_device,
        mesh=mesh,
        in_specs=(
            P(("groups", "fsdp", "tp"), None),
            P(("groups", "fsdp", "tp")),
            P("groups"),
            P(("groups", "fsdp", "tp"), None),
            P(("groups", "fsdp", "tp"), None),
            P(("groups", "fsdp", "tp"), None),
            P(("groups", "fsdp", "tp"), None),
            P("groups"),
            P("groups"),
            P("groups"),
        ),
        out_specs=P(("groups", "fsdp", "tp"), None),
        check_vma=False,
    )
```

```python
import functools

import jax
import jax.numpy as jnp
from jax import lax
from jax.experimental import pallas as pl
from jax.experimental.pallas import tpu as pltpu
from jax.sharding import PartitionSpec as P

HEAD = 128
LONGEST = 512
rope_base = 1000000.0
norm_eps = 1e-06
MASKED = -1e30
LOG2E = 1.4426950408889634
NOWHERE = 1 << 20
LEVEL = ("fsdp", "tp")


LIGHT = pl.CostEstimate(flops=1, bytes_accessed=1, transcendentals=0)
ROOM = pltpu.CompilerParams(vmem_limit_bytes=48 << 20)


def normalize(hidden, gain, order, n_f, depth, cuts):
    rows, width = hidden.shape
    n_t, cut = len(order), depth // cuts
    places = [(k, h, i) for k in range(n_t) for h in range(cuts) for i in range(n_f)]

    def scale(hidden):
        widened = hidden.astype(jnp.float32)
        return lax.rsqrt(jnp.mean(widened * widened, axis=-1, keepdims=True) + norm_eps)

    if cut % 128:
        normed = (hidden.astype(jnp.float32) * scale(hidden) * gain).astype(jnp.bfloat16)
        return jnp.concatenate([
            lax.dynamic_slice_in_dim(normed, (i * n_t + order[k]) * depth + h * cut, cut, 1)
            for k, h, i in places
        ], axis=1)

    def kernel(order_ref, hidden_ref, gain_ref, out_ref):
        factor = scale(hidden_ref[...])
        for place, (k, h, i) in enumerate(places):
            start = pl.multiple_of((i * n_t + order_ref[k]) * depth + h * cut, cut)
            span = pl.ds(start, cut)
            run = hidden_ref[:, span].astype(jnp.float32) * factor * gain_ref[:, span]
            out_ref[:, place * cut:(place + 1) * cut] = run.astype(jnp.bfloat16)

    block = min(64, rows)
    own = pl.BlockSpec((block, width), lambda m, order_ref: (m, 0))
    return pl.pallas_call(
        kernel,
        grid_spec=pltpu.PrefetchScalarGridSpec(
            num_scalar_prefetch=1,
            grid=(rows // block,),
            in_specs=[own, pl.BlockSpec((1, width), lambda m, order_ref: (0, 0))],
            out_specs=own,
        ),
        out_shape=jax.ShapeDtypeStruct(hidden.shape, jnp.bfloat16),
        compiler_params=ROOM,
        cost_estimate=LIGHT,
    )(jnp.stack(order).astype(jnp.int32), hidden, gain[None])


def segment_starts(segments):
    places = jnp.arange(segments.shape[-1], dtype=jnp.int32)
    same = segments[:, None] == segments[None, :]
    return jnp.min(jnp.where(same, places, segments.shape[-1]), axis=-1)


def rotary_tables(positions):
    half = HEAD // 2
    frequency = rope_base ** (-(jnp.arange(half, dtype=jnp.float32) * 2.0 / HEAD))
    angles = positions[:, None] * frequency[None, :]
    cosine, sine = jnp.cos(angles), jnp.sin(angles)
    return jnp.concatenate([cosine, cosine], -1), jnp.concatenate([-sine, sine], -1)


def attention_kernel(heads, scale, q_ref, bias_ref, cos_ref, sin_ref, start_ref, row_ref,
                     col_ref, k_ref, v_ref, out_ref):
    cosine, sine = cos_ref[...], sin_ref[...]
    columns = col_ref[...]
    allowed = (columns >= start_ref[...]) & (columns <= row_ref[...])
    keys, values = k_ref[0], v_ref[0]
    for head in range(heads):
        span = slice(head * HEAD, (head + 1) * HEAD)
        query = q_ref[:, span] + bias_ref[:, span]
        query = query * cosine + pltpu.roll(query, HEAD // 2, 1) * sine
        scores = lax.dot_general(
            query.astype(jnp.bfloat16), keys, (((1,), (1,)), ((), ())),
            preferred_element_type=jnp.float32,
        )
        scores = jnp.where(allowed, scores, MASKED)
        highest = jnp.max(scores, axis=-1, keepdims=True)
        weights = jnp.exp2((scores - highest) * (scale * LOG2E))
        share = 1.0 / jnp.sum(weights, axis=-1, keepdims=True)
        probs = (weights * share).astype(jnp.bfloat16)
        mixed = jnp.dot(probs, values, preferred_element_type=jnp.float32)
        out_ref[:, span] = mixed.astype(jnp.bfloat16)


def attention(part, *, rows, groups, width, f, projected, bias, cosine, sine, starts, row_ids,
              columns, key_value):
    n_keys = key_value.shape[1]
    mine = lambda g, f_ref: (2 * g + part, 0)

    def place(g, f_ref):
        d = g ^ f_ref[0]
        return (d // 2 + (d % 2) * (groups // 2), 0)

    def kernel(f_ref, *refs):
        attention_kernel(width // HEAD, HEAD ** -0.5, *refs)

    return pl.pallas_call(
        kernel,
        grid_spec=pltpu.PrefetchScalarGridSpec(
            num_scalar_prefetch=1,
            grid=(groups,),
            in_specs=[
                pl.BlockSpec((rows, width), mine),
                pl.BlockSpec((1, width), lambda g, f_ref: (0, 0)),
                pl.BlockSpec((rows, HEAD), mine),
                pl.BlockSpec((rows, HEAD), mine),
                pl.BlockSpec((rows, 1), mine),
                pl.BlockSpec((rows, 1), mine),
                pl.BlockSpec((1, n_keys), lambda g, f_ref: (0, 0)),
                pl.BlockSpec((1, n_keys, HEAD), lambda g, f_ref: (g, 0, 0)),
                pl.BlockSpec((1, n_keys, HEAD), lambda g, f_ref: (g, 0, 1)),
            ],
            out_specs=pl.BlockSpec((rows, width), place),
        ),
        out_shape=jax.ShapeDtypeStruct((groups * rows, width), jnp.bfloat16),
        compiler_params=ROOM,
        cost_estimate=LIGHT,
    )(jnp.full((1,), f, jnp.int32), projected, bias, cosine, sine, starts, row_ids, columns,
      key_value, key_value)


def project(tokens, weights, total=None, columns=None):
    n_rows, width = tokens.shape[0], weights[0].shape[1]
    block, n_w = min(512, n_rows), len(weights)
    first, width = (0, width) if columns is None else columns
    at = first // width

    def kernel(*refs):
        part, done = None, 0
        for ref in refs[1:1 + n_w]:
            depth = ref.shape[0]
            more = jnp.dot(
                refs[0][:, done:done + depth], ref[...], preferred_element_type=jnp.float32
            )
            part, done = more if part is None else part + more, done + depth
        refs[-1][...] = part if total is None else part + refs[1 + n_w][...]

    sums = pl.BlockSpec((block, width), lambda m: (m, at))
    return pl.pallas_call(
        kernel,
        grid=(n_rows // block,),
        in_specs=[pl.BlockSpec((block, tokens.shape[1]), lambda m: (m, 0))]
        + [pl.BlockSpec((w.shape[0], width), lambda m: (0, at)) for w in weights]
        + ([] if total is None else [sums]),
        out_specs=pl.BlockSpec((block, width), lambda m: (m, 0)),
        out_shape=jax.ShapeDtypeStruct((n_rows, width), jnp.float32),
        input_output_aliases={1 + n_w: 0} if total is not None and columns is None else {},
        compiler_params=ROOM,
        cost_estimate=LIGHT,
    )(tokens, *weights, *([] if total is None else [total]))


def times_transposed(left, right):
    return lax.dot_general(
        left, right, (((1,), (1,)), ((), ())), preferred_element_type=jnp.float32
    ).astype(jnp.bfloat16)


def partials_of_one(mixed, first, second, take_first):
    n_rows, depth = mixed.shape
    width = first.shape[0]
    block = n_rows // 2

    def kernel(take_ref, mixed_ref, first_ref, second_ref, kept_ref, given_ref):
        def multiply(weight_ref, out_ref):
            out_ref[...] = times_transposed(mixed_ref[...], weight_ref[...])

        for taken, weight_ref in ((1, first_ref), (0, second_ref)):
            for half, out_ref in enumerate((given_ref, kept_ref)):
                chosen = (take_ref[0] == taken) & (pl.program_id(0) == half)
                pl.when(chosen)(functools.partial(multiply, weight_ref, out_ref))

    whole = lambda m, take_ref: (0, 0)
    return pl.pallas_call(
        kernel,
        grid_spec=pltpu.PrefetchScalarGridSpec(
            num_scalar_prefetch=1,
            grid=(2,),
            in_specs=[
                pl.BlockSpec((block, depth), lambda m, take_ref: (1 - m, 0)),
                pl.BlockSpec((width, depth), whole),
                pl.BlockSpec((width, depth), whole),
            ],
            out_specs=[pl.BlockSpec((block, width), whole)] * 2,
        ),
        out_shape=[jax.ShapeDtypeStruct((block, width), jnp.bfloat16)] * 2,
        compiler_params=ROOM,
        cost_estimate=LIGHT,
    )(jnp.full((1,), take_first, jnp.int32), mixed, first, second)


def partials_of_two(mixed_a, mixed_b, weight):
    n_rows, depth = mixed_a.shape
    width = weight.shape[0]
    block = n_rows // 2

    def kernel(a_ref, b_ref, weight_ref, kept_ref, given_ref):
        step = pl.program_id(0)
        for place, mixed_ref in enumerate((a_ref, b_ref)):
            for half, out_ref in enumerate((given_ref, kept_ref)):
                def multiply(mixed_ref=mixed_ref, out_ref=out_ref):
                    out_ref[...] = times_transposed(mixed_ref[...], weight_ref[...])

                pl.when(step == 2 * half + place)(multiply)

    rows = pl.BlockSpec((block, depth), lambda m: (1 - m // 2, 0))
    return pl.pallas_call(
        kernel,
        grid=(4,),
        in_specs=[rows, rows, pl.BlockSpec((width, depth), lambda m: (0, 0))],
        out_specs=[
            pl.BlockSpec((block, width), lambda m: (0, jnp.maximum(m - 2, 0))),
            pl.BlockSpec((block, width), lambda m: (0, jnp.minimum(m, 1))),
        ],
        out_shape=[jax.ShapeDtypeStruct((block, 2 * width), jnp.bfloat16)] * 2,
        compiler_params=ROOM,
        cost_estimate=LIGHT,
    )(mixed_a, mixed_b, weight)


def add_up(result, hidden, terms, item, other, other_item, use_terms, count, level, n_t, cuts, cut, h, first):
    rows = result.shape[0]
    wide = lambda term: term.astype(jnp.float32)
    if cut % 128:
        total = sum(wide(term[item, :rows, :count * cut]) for term in terms)
        if other is not None:
            total = jnp.where(use_terms, total, wide(other[other_item]))
        for i in range(count):
            column = ((first + i) * n_t + level) * cuts * cut + h * cut
            before = wide(lax.dynamic_slice_in_dim(hidden, column, cut, 1))
            result = lax.dynamic_update_slice_in_dim(
                result, (before + total[:, i * cut:(i + 1) * cut]).astype(jnp.bfloat16), column, 1)
        return result

    def kernel(at_ref, result_ref, hidden_ref, *refs):
        total = sum(wide(ref[...]) for ref in refs[:len(terms)])
        if other is not None:
            total = jnp.where(at_ref[1] == 1, total, wide(refs[len(terms)][...]))
        refs[-1][...] = (wide(hidden_ref[...]) + total).astype(jnp.bfloat16)

    place = pl.BlockSpec(
        (rows, cut), lambda i, at_ref: (0, ((first + i) * n_t + at_ref[0]) * cuts + h))
    one = lambda item: pl.BlockSpec((None, rows, cut), lambda i, at_ref: (item, 0, i))
    extra = [] if other is None else [other]
    return pl.pallas_call(
        kernel,
        grid_spec=pltpu.PrefetchScalarGridSpec(
            num_scalar_prefetch=1,
            grid=(count,),
            in_specs=[pl.BlockSpec(memory_space=pl.ANY), place]
            + [one(item)] * len(terms) + [one(other_item)] * len(extra),
            out_specs=place,
        ),
        out_shape=jax.ShapeDtypeStruct(result.shape, result.dtype),
        input_output_aliases={1: 0},
        compiler_params=ROOM,
        cost_estimate=LIGHT,
    )(jnp.stack([level, use_terms.astype(jnp.int32)]), result, hidden, *terms, *extra)


def per_device(
    hidden_in,
    segment_ids,
    norm_gain,
    query_weight,
    key_weight,
    value_weight,
    output_weight,
    query_bias,
    key_bias,
    value_bias,
):
    n_f, n_t = lax.axis_size("fsdp"), lax.axis_size("tp")
    f, t = lax.axis_index("fsdp"), lax.axis_index("tp")
    rows, width = hidden_in.shape
    depth = query_weight.shape[0]
    q_cols = query_weight.shape[1] // n_f
    kv_heads = key_weight.shape[1] // HEAD
    kv_head = f * kv_heads // n_f
    cuts = max(1, depth // 256)
    cut = depth // cuts
    n_pairs = n_t // 2
    inner = [2 * j + 1 - j % 2 for j in range(n_pairs)]
    outer = [2 * j + j % 2 for j in range(n_pairs)]
    pair = t // 2
    my_inner = 2 * pair + 1 - pair % 2
    my_outer = 2 * pair + pair % 2
    is_inner = t == my_inner
    inward = [(outer[j], inner[j]) for j in range(n_pairs)]
    outward = [(inner[j], outer[j]) for j in range(n_pairs)]
    every = list(range(n_t))
    tie = lax.optimization_barrier

    def shift(s):
        return [(inner[(j + s) % n_pairs], inner[j]) for j in range(n_pairs)]

    def send(value, pairs):
        return lax.ppermute(value, "tp", pairs)

    def swap(value, d, levels):
        return lax.ppermute(value, LEVEL, [
            (i * n_t + z, (i ^ d) * n_t + z) for i in range(n_f) for z in levels
        ])

    order = []
    for s in range(n_pairs):
        p = (pair + s) % n_pairs
        order += [2 * p + 1 - p % 2, 2 * p + p % 2]

    def by_index(pieces):
        bit = 1
        while bit < n_f:
            here = (f & bit) != 0
            pieces = [jnp.where(here, pieces[d ^ bit], pieces[d]) for d in range(n_f)]
            bit *= 2
        return jnp.concatenate(pieces, axis=0)

    def level_exchange(block_for, levels):
        return by_index([block_for(f)] + [
            swap(block_for(f ^ d), d, levels) for d in range(1, n_f)
        ])

    def projection_block(weights, h):
        def block(c):
            head = c * kv_heads // n_f
            span = slice(h * cut, (h + 1) * cut)
            return jnp.concatenate([
                lax.dynamic_slice_in_dim(weights[0][span], c * q_cols, q_cols, 1),
                lax.dynamic_slice_in_dim(weights[1][span], head * HEAD, HEAD, 1),
                lax.dynamic_slice_in_dim(weights[2][span], head * HEAD, HEAD, 1),
            ], axis=1)
        return block

    segments = lax.all_gather(segment_ids, "tp", axis=0, tiled=True)
    segments, hidden, output_weight, weights = tie(
        (segments, hidden_in, output_weight, (query_weight, key_weight, value_weight)))
    my_starts = lax.dynamic_slice_in_dim(segment_starts(segments), t * rows, rows)
    digits = jnp.stack([my_starts // 256, my_starts % 256], axis=1).astype(jnp.bfloat16)
    digits = jnp.pad(digits, ((0, 0), (0, HEAD - 2)))

    mine = normalize(hidden, norm_gain, order, n_f, depth, cuts)
    part = n_f * depth

    def gather(k, theirs, outputs):
        both = jnp.concatenate([mine[:, k * part:(k + 1) * part], theirs], axis=0)
        chunks = outputs.shape[1] // part
        outputs = jnp.concatenate(
            [outputs[:, c * part:(c + 1) * part] for c in range(chunks)], axis=0)
        payload = jnp.where(is_inner, both, outputs)
        if k == 0:
            payload = jnp.concatenate(
                [payload, jnp.concatenate([digits, their_digits], axis=0)], axis=1)
        return lax.all_gather(payload, "fsdp", axis=0, tiled=True)

    def output_rows(gathered, count):
        blocks = gathered.reshape(n_f, -1, count, gathered.shape[1])
        column = f * q_cols
        blocks = lax.dynamic_slice(
            blocks, (0, column // part, 0, column % part), (n_f, 1, count, q_cols))
        return blocks.reshape(n_f, count, q_cols)

    count = 2 * rows * part // output_weight.shape[1]
    early = part

    own = [level_exchange(projection_block(weights, 0), every)]
    head = send(jnp.concatenate([mine[:, :early], digits], axis=1), inward)
    tail = send(mine[:, early:], inward)
    own, weights = tie((own, weights))
    their_digits = head[:, early:]
    raw = []

    def source(k):
        runs = cut // count
        run, at = k // runs, (k % runs) * count
        if run >= 2 * cuts:
            return jnp.zeros((count, output_weight.shape[1]), output_weight.dtype)
        some = raw[run - cuts] if run >= cuts else output_weight[run * cut:(run + 1) * cut]
        return some[at:at + count]

    across = [send(own[0], shift(1))] if n_pairs > 1 else []
    own += [level_exchange(projection_block(weights, h), every) for h in range(1, cuts)]
    gathered = [gather(0, tie((head, own[0]))[0][:, :part], source(0))]
    own, across, tail, mine, output_weight = tie((own, across, tail, mine, output_weight))
    theirs = jnp.concatenate([head[:, :early], tail], axis=1)

    beyond = []
    projected = None
    for h in range(cuts):
        until = min(n_t, (cuts + h) * (cut // count))
        gathered += [
            gather(k, theirs[:, k * part:(k + 1) * part], source(k))
            for k in range(len(gathered), until)
        ]
        if n_pairs > 1 and h + 1 < cuts:
            across.append(send(own[h + 1], shift(1)))
        elif n_pairs > 1 and h:
            across.append(send(beyond[0], shift(1)))
        beyond.append(send(own[h], inward))
        raw.append(send(output_weight[h * cut:(h + 1) * cut], outward))
        if h == 0:
            projected = project(gathered[0], own)
        own, beyond, across, raw, output_weight, projected, theirs, mine = tie(
            (own, beyond, across, raw, output_weight, projected, theirs, mine))
    gathered += [
        gather(k, theirs[:, k * part:(k + 1) * part], source(k)) for k in range(len(gathered), n_t)
    ]

    def outer_run(r):
        return jnp.concatenate([
            output_rows(gathered[k], count)
            for k in range(r * (cut // count), (r + 1) * (cut // count))
        ], axis=1).reshape(-1, q_cols)

    at_outer = [outer_run(0)]
    at_inner = [send(at_outer[0], inward)]
    if n_pairs > 1:
        across += [send(w, shift(1)) for w in beyond[len(across) - cuts:]]
    waiting = [(1, beyond)]
    if n_pairs > 1:
        projected = project(gathered[1], beyond, projected)
        projected = project(gathered[2], across[:cuts], projected)
        waiting = [(3, across[cuts:])]
    projected, across, at_inner, at_outer = tie((projected, across, at_inner, at_outer))

    groups = []
    half = n_f // 2
    for s in range(1, n_pairs):
        halves = [(s, r, p) for r in range(2 * cuts) for p in range(2)]
        groups += [halves[i:i + 2] for i in range(0, len(halves), 2)]

    def send_group(group):
        return send(jnp.concatenate([
            at_inner[r][p * half * cut:(p + 1) * half * cut] for _, r, p in group
        ], axis=0), shift(group[0][0]))

    arrived = {}

    def arrive(group, got):
        for place, (s, r, p) in enumerate(group):
            arrived[s, r, p] = got[place * half * cut:(place + 1) * half * cut]

    for s in range(2, n_pairs):
        across = [send(w, shift(s)) for w in own + beyond]
        waiting += [(2 * s, across[:cuts]), (2 * s + 1, across[cuts:])]
    for k, some in waiting[:-1]:
        projected = project(gathered[k], some, projected)
    k, some = waiting[-1]
    projected_pair = project(gathered[k], some, projected, (q_cols, 2 * HEAD))
    projected_queries = project(gathered[k], some, projected, (0, q_cols))

    level_ids = jnp.arange(rows, dtype=jnp.int32)
    pair_ids = jnp.concatenate([my_inner * rows + level_ids, my_outer * rows + level_ids])
    row_ids = jnp.tile(pair_ids, n_f)
    digits = gathered[0][:, part:part + 2].astype(jnp.int32)
    starts = digits[:, 0] * 256 + digits[:, 1]
    cosine, sine = rotary_tables((row_ids - starts).astype(jnp.float32))

    key_rows = projected_pair[:, :HEAD]
    key_rows = key_rows + lax.dynamic_slice_in_dim(key_bias, kv_head * HEAD, HEAD)
    turned = jnp.concatenate([key_rows[:, HEAD // 2:], key_rows[:, :HEAD // 2]], axis=-1)
    keys = (key_rows * cosine + turned * sine).astype(jnp.bfloat16)
    values = projected_pair[:, HEAD:] + lax.dynamic_slice_in_dim(value_bias, kv_head * HEAD, HEAD)
    values = values.astype(jnp.bfloat16)
    pair_rows = 2 * rows
    key_value = jnp.concatenate(
        [keys.reshape(n_f, pair_rows, HEAD), values.reshape(n_f, pair_rows, HEAD)], axis=-1
    )
    seen = [key_value]
    reach = min(n_t - 1, -(-(LONGEST - 1) // rows))
    for s in range(1, min(n_pairs - 1, (reach + 1) // 2) + 1):
        seen.append(send(key_value, [(inner[j - s], inner[j]) for j in range(s, n_pairs)]))
    if groups:
        at_inner[0] = tie((at_inner[0], seen[1]))[0]
    got = send_group(groups[0]) if groups else None
    if len(at_inner) < 2 * cuts:
        at_outer.append(outer_run(1))
        at_inner.append(send(at_outer[1], inward))

    def attend(outer_rows):
        blocks, columns = [], []
        for d in range(reach + 1):
            found = []
            for parity in range(2):
                offset = (1 - parity) ^ outer_rows
                s = -((offset - d) // 2)
                place = ((offset - d) % 2) ^ (1 - (parity + s) % 2)
                block = seen[s] if s < len(seen) else jnp.zeros_like(key_value)
                found.append(block[:, place * rows:(place + 1) * rows])
            blocks.append(jnp.where(pair % 2 == 0, found[0], found[1]))
            level = (my_outer if outer_rows else my_inner) - d
            columns.append(jnp.where(level >= 0, level * rows + level_ids, NOWHERE))
        return attention(
            outer_rows, rows=rows, groups=n_f, width=q_cols, f=f, projected=projected_queries,
            bias=lax.dynamic_slice_in_dim(query_bias, f * q_cols, q_cols)[None],
            cosine=cosine, sine=sine, starts=starts[:, None], row_ids=row_ids[:, None],
            columns=jnp.concatenate(columns)[None], key_value=jnp.concatenate(blocks, axis=1),
        )

    wide = lambda value: value.astype(jnp.float32)

    def multiply(item):
        if item[0] == 0:
            return partials_of_one(mixed, at_inner[item[1]], at_outer[item[1]], is_inner)
        return partials_of_two(mixed_inner, mixed_outer, arrived[item])

    def between_cores(items, long_ones):
        kept, given = [], []
        for item in items:
            if item == (0, 2 * cuts - 1) and kept:
                at_inner[-1], kept[-1] = tie((at_inner[-1], kept[-1]))
            a, b = multiply(item)
            kept, given = kept + [a], given + [b]
        given = tie((jnp.stack(given), long_ones))[0]
        return items, jnp.stack(kept), swap(given, 1, every)

    def between_chips(items, kept, given):
        crossed = []
        for d in range(2, n_f, 2):
            span = slice(d // 2 * rows, (d // 2 + 1) * rows)
            share = wide(kept[:, span]) + wide(given[:, span])
            crossed.append(swap(share.astype(jnp.bfloat16), d, every))
        return items, [kept, given] + crossed

    def between_levels(items, terms):
        others = [i for i, item in enumerate(items) if item[0]]
        if not others:
            return items, terms, None
        sums = [
            sum(wide(term[i, :rows, half * cut:]) for term in terms).astype(jnp.bfloat16)
            for i in others
        ]
        return items, terms, send(jnp.stack(sums), outward)

    def put(result, items, terms, other):
        n_other = 0
        for i, item in enumerate(items):
            level, h = 1 - item[1] // cuts, item[1] % cuts
            if item[0] == 0:
                result = add_up(
                    result, hidden_in, terms, i, None, 0, is_inner, n_f, order[level],
                    n_t, cuts, cut, h, 0)
            else:
                result = add_up(
                    result, hidden_in, terms, i, other, n_other, is_inner, half,
                    order[2 * item[0] + level], n_t, cuts, cut, h, item[2] * half)
                n_other += 1
        return result

    mixed_outer = attend(1)
    mixed_outer, at_inner, at_outer, projected_queries, seen = tie(
        (mixed_outer, at_inner, at_outer, projected_queries, seen))
    if groups:
        arrive(groups[0], got)
    runs = [(0, r) for r in range(2 * cuts)]
    result, phase, from_cores, from_chips, from_levels = hidden_in, 1, None, None, None
    while phase <= len(groups) or runs or from_cores or from_chips or from_levels:
        got = send_group(groups[phase]) if phase < len(groups) else None
        if len(at_inner) < 2 * cuts:
            at_outer.append(outer_run(len(at_inner)))
            at_inner.append(send(at_outer[-1], inward))
        received = from_levels
        from_levels = between_levels(*from_chips) if from_chips else None
        from_chips = between_chips(*from_cores) if from_cores else None
        if phase == 1:
            there = send(mixed_outer, outward)
            mixed_inner = attend(0)
            mixed = jnp.where(is_inner, mixed_inner, there)
        items = list(groups[phase - 1]) if phase <= len(groups) else []
        ready = runs[:cuts]
        items, runs = items + ready, runs[cuts:]
        long_ones = (got, at_inner[-1:], from_chips and from_chips[1], from_levels and from_levels[2], there)
        from_cores = between_cores(items, long_ones) if items else None
        if received:
            result = put(result, *received)
        moving = [None if x is None else x[1:] for x in (from_cores, from_chips, from_levels)]
        moving, got, at_inner, at_outer, result = tie((moving, got, at_inner, at_outer, result))
        from_cores, from_chips, from_levels = [
            None if x is None else (x[0],) + tuple(y)
            for x, y in zip((from_cores, from_chips, from_levels), moving)
        ]
        if got is not None:
            arrive(groups[phase], got)
        phase += 1
    return result


def solution(mesh):
    return jax.shard_map(
        per_device,
        mesh=mesh,
        in_specs=(
            P(("groups", "fsdp", "tp"), None),
            P(("groups", "fsdp", "tp")),
            P("groups"),
            P(("groups", "fsdp", "tp"), None),
            P(("groups", "fsdp", "tp"), None),
            P(("groups", "fsdp", "tp"), None),
            P(("groups", "fsdp", "tp"), None),
            P("groups"),
            P("groups"),
            P("groups"),
        ),
        out_specs=P(("groups", "fsdp", "tp"), None),
        check_vma=False,
    )
```

```python
import functools

import jax
import jax.numpy as jnp
from jax import lax
from jax.experimental import pallas as pl
from jax.experimental.pallas import tpu as pltpu
from jax.sharding import PartitionSpec as P

HEAD = 128
LONGEST = 512
rope_base = 1000000.0
norm_eps = 1e-06
MASKED = -1e30
LOG2E = 1.4426950408889634
NOWHERE = 1 << 20
LEVEL = ("fsdp", "tp")


LIGHT = pl.CostEstimate(flops=1, bytes_accessed=1, transcendentals=0)
ROOM = pltpu.CompilerParams(vmem_limit_bytes=48 << 20)


def normalize(hidden, gain, order, n_f, depth, cuts):
    rows, width = hidden.shape
    n_t, cut = len(order), depth // cuts
    places = [(k, h, i) for k in range(n_t) for h in range(cuts) for i in range(n_f)]

    def scale(hidden):
        widened = hidden.astype(jnp.float32)
        return lax.rsqrt(jnp.mean(widened * widened, axis=-1, keepdims=True) + norm_eps)

    if cut % 128:
        normed = (hidden.astype(jnp.float32) * scale(hidden) * gain).astype(jnp.bfloat16)
        return jnp.concatenate([
            lax.dynamic_slice_in_dim(normed, (i * n_t + order[k]) * depth + h * cut, cut, 1)
            for k, h, i in places
        ], axis=1)

    def kernel(order_ref, hidden_ref, gain_ref, out_ref):
        factor = scale(hidden_ref[...])
        for place, (k, h, i) in enumerate(places):
            start = pl.multiple_of((i * n_t + order_ref[k]) * depth + h * cut, cut)
            span = pl.ds(start, cut)
            run = hidden_ref[:, span].astype(jnp.float32) * factor * gain_ref[:, span]
            out_ref[:, place * cut:(place + 1) * cut] = run.astype(jnp.bfloat16)

    block = min(64, rows)
    own = pl.BlockSpec((block, width), lambda m, order_ref: (m, 0))
    return pl.pallas_call(
        kernel,
        grid_spec=pltpu.PrefetchScalarGridSpec(
            num_scalar_prefetch=1,
            grid=(rows // block,),
            in_specs=[own, pl.BlockSpec((1, width), lambda m, order_ref: (0, 0))],
            out_specs=own,
        ),
        out_shape=jax.ShapeDtypeStruct(hidden.shape, jnp.bfloat16),
        compiler_params=ROOM,
        cost_estimate=LIGHT,
    )(jnp.stack(order).astype(jnp.int32), hidden, gain[None])


def segment_starts(segments):
    places = jnp.arange(segments.shape[-1], dtype=jnp.int32)
    same = segments[:, None] == segments[None, :]
    return jnp.min(jnp.where(same, places, segments.shape[-1]), axis=-1)


def rotary_tables(positions):
    half = HEAD // 2
    frequency = rope_base ** (-(jnp.arange(half, dtype=jnp.float32) * 2.0 / HEAD))
    angles = positions[:, None] * frequency[None, :]
    cosine, sine = jnp.cos(angles), jnp.sin(angles)
    return jnp.concatenate([cosine, cosine], -1), jnp.concatenate([-sine, sine], -1)


def attention_kernel(heads, scale, q_ref, bias_ref, cos_ref, sin_ref, start_ref, row_ref,
                     col_ref, k_ref, v_ref, out_ref):
    cosine, sine = cos_ref[...], sin_ref[...]
    columns = col_ref[...]
    allowed = (columns >= start_ref[...]) & (columns <= row_ref[...])
    keys, values = k_ref[0], v_ref[0]
    for head in range(heads):
        span = slice(head * HEAD, (head + 1) * HEAD)
        query = q_ref[:, span] + bias_ref[:, span]
        query = query * cosine + pltpu.roll(query, HEAD // 2, 1) * sine
        scores = lax.dot_general(
            query.astype(jnp.bfloat16), keys, (((1,), (1,)), ((), ())),
            preferred_element_type=jnp.float32,
        )
        scores = jnp.where(allowed, scores, MASKED)
        highest = jnp.max(scores, axis=-1, keepdims=True)
        weights = jnp.exp2((scores - highest) * (scale * LOG2E))
        share = 1.0 / jnp.sum(weights, axis=-1, keepdims=True)
        probs = (weights * share).astype(jnp.bfloat16)
        mixed = jnp.dot(probs, values, preferred_element_type=jnp.float32)
        out_ref[:, span] = mixed.astype(jnp.bfloat16)


def attention(part, *, rows, groups, width, f, projected, bias, cosine, sine, starts, row_ids,
              columns, key_value):
    n_keys = key_value.shape[1]
    mine = lambda g, f_ref: (2 * g + part, 0)

    def place(g, f_ref):
        d = g ^ f_ref[0]
        return (d // 2 + (d % 2) * (groups // 2), 0)

    def kernel(f_ref, *refs):
        attention_kernel(width // HEAD, HEAD ** -0.5, *refs)

    return pl.pallas_call(
        kernel,
        grid_spec=pltpu.PrefetchScalarGridSpec(
            num_scalar_prefetch=1,
            grid=(groups,),
            in_specs=[
                pl.BlockSpec((rows, width), mine),
                pl.BlockSpec((1, width), lambda g, f_ref: (0, 0)),
                pl.BlockSpec((rows, HEAD), mine),
                pl.BlockSpec((rows, HEAD), mine),
                pl.BlockSpec((rows, 1), mine),
                pl.BlockSpec((rows, 1), mine),
                pl.BlockSpec((1, n_keys), lambda g, f_ref: (0, 0)),
                pl.BlockSpec((1, n_keys, HEAD), lambda g, f_ref: (g, 0, 0)),
                pl.BlockSpec((1, n_keys, HEAD), lambda g, f_ref: (g, 0, 1)),
            ],
            out_specs=pl.BlockSpec((rows, width), place),
        ),
        out_shape=jax.ShapeDtypeStruct((groups * rows, width), jnp.bfloat16),
        compiler_params=ROOM,
        cost_estimate=LIGHT,
    )(jnp.full((1,), f, jnp.int32), projected, bias, cosine, sine, starts, row_ids, columns,
      key_value, key_value)


def project(tokens, weights, total=None, columns=None):
    n_rows, width = tokens.shape[0], weights[0].shape[1]
    block, n_w = min(512, n_rows), len(weights)
    first, width = (0, width) if columns is None else columns
    at = first // width

    def kernel(*refs):
        part, done = None, 0
        for ref in refs[1:1 + n_w]:
            depth = ref.shape[0]
            more = jnp.dot(
                refs[0][:, done:done + depth], ref[...], preferred_element_type=jnp.float32
            )
            part, done = more if part is None else part + more, done + depth
        refs[-1][...] = part if total is None else part + refs[1 + n_w][...]

    sums = pl.BlockSpec((block, width), lambda m: (m, at))
    return pl.pallas_call(
        kernel,
        grid=(n_rows // block,),
        in_specs=[pl.BlockSpec((block, tokens.shape[1]), lambda m: (m, 0))]
        + [pl.BlockSpec((w.shape[0], width), lambda m: (0, at)) for w in weights]
        + ([] if total is None else [sums]),
        out_specs=pl.BlockSpec((block, width), lambda m: (m, 0)),
        out_shape=jax.ShapeDtypeStruct((n_rows, width), jnp.float32),
        input_output_aliases={1 + n_w: 0} if total is not None and columns is None else {},
        compiler_params=ROOM,
        cost_estimate=LIGHT,
    )(tokens, *weights, *([] if total is None else [total]))


def times_transposed(left, right):
    return lax.dot_general(
        left, right, (((1,), (1,)), ((), ())), preferred_element_type=jnp.float32
    ).astype(jnp.bfloat16)


def partials_of_one(mixed, first, second, take_first):
    n_rows, depth = mixed.shape
    width = first.shape[0]
    block = n_rows // 2

    def kernel(take_ref, mixed_ref, first_ref, second_ref, kept_ref, given_ref):
        def multiply(weight_ref, out_ref):
            out_ref[...] = times_transposed(mixed_ref[...], weight_ref[...])

        for taken, weight_ref in ((1, first_ref), (0, second_ref)):
            for half, out_ref in enumerate((given_ref, kept_ref)):
                chosen = (take_ref[0] == taken) & (pl.program_id(0) == half)
                pl.when(chosen)(functools.partial(multiply, weight_ref, out_ref))

    whole = lambda m, take_ref: (0, 0)
    return pl.pallas_call(
        kernel,
        grid_spec=pltpu.PrefetchScalarGridSpec(
            num_scalar_prefetch=1,
            grid=(2,),
            in_specs=[
                pl.BlockSpec((block, depth), lambda m, take_ref: (1 - m, 0)),
                pl.BlockSpec((width, depth), whole),
                pl.BlockSpec((width, depth), whole),
            ],
            out_specs=[pl.BlockSpec((block, width), whole)] * 2,
        ),
        out_shape=[jax.ShapeDtypeStruct((block, width), jnp.bfloat16)] * 2,
        compiler_params=ROOM,
        cost_estimate=LIGHT,
    )(jnp.full((1,), take_first, jnp.int32), mixed, first, second)


def partials_of_two(mixed_a, mixed_b, weight):
    n_rows, depth = mixed_a.shape
    width = weight.shape[0]
    block = n_rows // 2

    def kernel(a_ref, b_ref, weight_ref, kept_ref, given_ref):
        step = pl.program_id(0)
        for place, mixed_ref in enumerate((a_ref, b_ref)):
            for half, out_ref in enumerate((given_ref, kept_ref)):
                def multiply(mixed_ref=mixed_ref, out_ref=out_ref):
                    out_ref[...] = times_transposed(mixed_ref[...], weight_ref[...])

                pl.when(step == 2 * half + place)(multiply)

    rows = pl.BlockSpec((block, depth), lambda m: (1 - m // 2, 0))
    return pl.pallas_call(
        kernel,
        grid=(4,),
        in_specs=[rows, rows, pl.BlockSpec((width, depth), lambda m: (0, 0))],
        out_specs=[
            pl.BlockSpec((block, width), lambda m: (0, jnp.maximum(m - 2, 0))),
            pl.BlockSpec((block, width), lambda m: (0, jnp.minimum(m, 1))),
        ],
        out_shape=[jax.ShapeDtypeStruct((block, 2 * width), jnp.bfloat16)] * 2,
        compiler_params=ROOM,
        cost_estimate=LIGHT,
    )(mixed_a, mixed_b, weight)


def add_up(result, hidden, terms, item, other, other_item, use_terms, count, level, n_t, cuts, cut, h, first):
    rows = result.shape[0]
    wide = lambda term: term.astype(jnp.float32)
    if cut % 128:
        total = sum(wide(term[item, :rows, :count * cut]) for term in terms)
        if other is not None:
            total = jnp.where(use_terms, total, wide(other[other_item]))
        for i in range(count):
            column = ((first + i) * n_t + level) * cuts * cut + h * cut
            before = wide(lax.dynamic_slice_in_dim(hidden, column, cut, 1))
            result = lax.dynamic_update_slice_in_dim(
                result, (before + total[:, i * cut:(i + 1) * cut]).astype(jnp.bfloat16), column, 1)
        return result

    def kernel(at_ref, result_ref, hidden_ref, *refs):
        total = sum(wide(ref[...]) for ref in refs[:len(terms)])
        if other is not None:
            total = jnp.where(at_ref[1] == 1, total, wide(refs[len(terms)][...]))
        refs[-1][...] = (wide(hidden_ref[...]) + total).astype(jnp.bfloat16)

    place = pl.BlockSpec(
        (rows, cut), lambda i, at_ref: (0, ((first + i) * n_t + at_ref[0]) * cuts + h))
    one = lambda item: pl.BlockSpec((None, rows, cut), lambda i, at_ref: (item, 0, i))
    extra = [] if other is None else [other]
    return pl.pallas_call(
        kernel,
        grid_spec=pltpu.PrefetchScalarGridSpec(
            num_scalar_prefetch=1,
            grid=(count,),
            in_specs=[pl.BlockSpec(memory_space=pl.ANY), place]
            + [one(item)] * len(terms) + [one(other_item)] * len(extra),
            out_specs=place,
        ),
        out_shape=jax.ShapeDtypeStruct(result.shape, result.dtype),
        input_output_aliases={1: 0},
        compiler_params=ROOM,
        cost_estimate=LIGHT,
    )(jnp.stack([level, use_terms.astype(jnp.int32)]), result, hidden, *terms, *extra)


def per_device(
    hidden_in,
    segment_ids,
    norm_gain,
    query_weight,
    key_weight,
    value_weight,
    output_weight,
    query_bias,
    key_bias,
    value_bias,
):
    n_f, n_t = lax.axis_size("fsdp"), lax.axis_size("tp")
    f, t = lax.axis_index("fsdp"), lax.axis_index("tp")
    rows, width = hidden_in.shape
    depth = query_weight.shape[0]
    q_cols = query_weight.shape[1] // n_f
    kv_heads = key_weight.shape[1] // HEAD
    kv_head = f * kv_heads // n_f
    cuts = max(1, depth // 256)
    cut = depth // cuts
    n_pairs = n_t // 2
    inner = [2 * j + 1 - j % 2 for j in range(n_pairs)]
    outer = [2 * j + j % 2 for j in range(n_pairs)]
    pair = t // 2
    my_inner = 2 * pair + 1 - pair % 2
    my_outer = 2 * pair + pair % 2
    is_inner = t == my_inner
    inward = [(outer[j], inner[j]) for j in range(n_pairs)]
    outward = [(inner[j], outer[j]) for j in range(n_pairs)]
    every = list(range(n_t))
    tie = lax.optimization_barrier

    def shift(s):
        return [(inner[(j + s) % n_pairs], inner[j]) for j in range(n_pairs)]

    def send(value, pairs):
        return lax.ppermute(value, "tp", pairs)

    def swap(value, d, levels):
        return lax.ppermute(value, LEVEL, [
            (i * n_t + z, (i ^ d) * n_t + z) for i in range(n_f) for z in levels
        ])

    order = []
    for s in range(n_pairs):
        p = (pair + s) % n_pairs
        order += [2 * p + 1 - p % 2, 2 * p + p % 2]

    def by_index(pieces):
        bit = 1
        while bit < n_f:
            here = (f & bit) != 0
            pieces = [jnp.where(here, pieces[d ^ bit], pieces[d]) for d in range(n_f)]
            bit *= 2
        return jnp.concatenate(pieces, axis=0)

    def level_exchange(block_for, levels):
        return by_index([block_for(f)] + [
            swap(block_for(f ^ d), d, levels) for d in range(1, n_f)
        ])

    def projection_block(weights, h):
        def block(c):
            head = c * kv_heads // n_f
            span = slice(h * cut, (h + 1) * cut)
            return jnp.concatenate([
                lax.dynamic_slice_in_dim(weights[0][span], c * q_cols, q_cols, 1),
                lax.dynamic_slice_in_dim(weights[1][span], head * HEAD, HEAD, 1),
                lax.dynamic_slice_in_dim(weights[2][span], head * HEAD, HEAD, 1),
            ], axis=1)
        return block

    weights = (query_weight, key_weight, value_weight)
    mine = normalize(hidden_in, norm_gain, order, n_f, depth, cuts)
    part = n_f * depth

    def gather(k, theirs, outputs):
        both = jnp.concatenate([mine[:, k * part:(k + 1) * part], theirs], axis=0)
        chunks = outputs.shape[1] // part
        outputs = jnp.concatenate(
            [outputs[:, c * part:(c + 1) * part] for c in range(chunks)], axis=0)
        payload = jnp.where(is_inner, both, outputs)
        if k == 1:
            payload = jnp.concatenate(
                [payload, jnp.concatenate([digits, tail[:, width - early:]], axis=0)], axis=1)
        return lax.all_gather(payload, "fsdp", axis=0, tiled=True)

    def output_rows(gathered, count):
        blocks = gathered.reshape(n_f, -1, count, gathered.shape[1])
        column = f * q_cols
        blocks = lax.dynamic_slice(
            blocks, (0, column // part, 0, column % part), (n_f, 1, count, q_cols))
        return blocks.reshape(n_f, count, q_cols)

    count = 2 * rows * part // output_weight.shape[1]
    early = part

    own = [level_exchange(projection_block(weights, 0), every)]
    head = send(mine[:, :early], inward)
    own, weights, segment_ids = tie((own, weights, segment_ids))

    segments = lax.all_gather(segment_ids, "tp", axis=0, tiled=True)
    own, segments = tie((own, segments))
    my_starts = lax.dynamic_slice_in_dim(segment_starts(segments), t * rows, rows)
    digits = jnp.stack([my_starts // 256, my_starts % 256], axis=1).astype(jnp.bfloat16)
    digits = jnp.pad(digits, ((0, 0), (0, HEAD - 2)))
    tail = send(jnp.concatenate([mine[:, early:], digits], axis=1), inward)
    raw = []

    def source(k):
        runs = cut // count
        run, at = k // runs, (k % runs) * count
        if run >= 2 * cuts:
            return jnp.zeros((count, output_weight.shape[1]), output_weight.dtype)
        some = raw[run - cuts] if run >= cuts else output_weight[run * cut:(run + 1) * cut]
        return some[at:at + count]

    across = [send(own[0], shift(1))] if n_pairs > 1 else []
    own += [level_exchange(projection_block(weights, h), every) for h in range(1, cuts)]
    gathered = [gather(0, tie((head, own[0]))[0][:, :part], source(0))]
    own, across, tail, mine, output_weight = tie((own, across, tail, mine, output_weight))
    theirs = jnp.concatenate([head, tail[:, :width - early]], axis=1)

    beyond = []
    projected = None
    for h in range(cuts):
        until = min(n_t, (cuts + h) * (cut // count))
        gathered += [
            gather(k, theirs[:, k * part:(k + 1) * part], source(k))
            for k in range(len(gathered), until)
        ]
        if n_pairs > 1 and h + 1 < cuts:
            across.append(send(own[h + 1], shift(1)))
        elif n_pairs > 1 and h:
            across.append(send(beyond[0], shift(1)))
        beyond.append(send(own[h], inward))
        raw.append(send(output_weight[h * cut:(h + 1) * cut], outward))
        if h == 0:
            projected = project(gathered[0], own)
        own, beyond, across, raw, output_weight, projected, theirs, mine = tie(
            (own, beyond, across, raw, output_weight, projected, theirs, mine))
    gathered += [
        gather(k, theirs[:, k * part:(k + 1) * part], source(k)) for k in range(len(gathered), n_t)
    ]

    def outer_run(r):
        return jnp.concatenate([
            output_rows(gathered[k], count)
            for k in range(r * (cut // count), (r + 1) * (cut // count))
        ], axis=1).reshape(-1, q_cols)

    at_outer = [outer_run(0)]
    at_inner = [send(at_outer[0], inward)]
    if n_pairs > 1:
        across += [send(w, shift(1)) for w in beyond[len(across) - cuts:]]
    waiting = [(1, beyond)]
    if n_pairs > 1:
        projected = project(gathered[1], beyond, projected)
        projected = project(gathered[2], across[:cuts], projected)
        waiting = [(3, across[cuts:])]
    projected, across, at_inner, at_outer = tie((projected, across, at_inner, at_outer))

    groups = []
    half = n_f // 2
    for s in range(1, n_pairs):
        halves = [(s, r, p) for r in range(2 * cuts) for p in range(2)]
        groups += [halves[i:i + 2] for i in range(0, len(halves), 2)]

    def send_group(group):
        return send(jnp.concatenate([
            at_inner[r][p * half * cut:(p + 1) * half * cut] for _, r, p in group
        ], axis=0), shift(group[0][0]))

    arrived = {}

    def arrive(group, got):
        for place, (s, r, p) in enumerate(group):
            arrived[s, r, p] = got[place * half * cut:(place + 1) * half * cut]

    for s in range(2, n_pairs):
        across = [send(w, shift(s)) for w in own + beyond]
        waiting += [(2 * s, across[:cuts]), (2 * s + 1, across[cuts:])]
    for k, some in waiting[:-1]:
        projected = project(gathered[k], some, projected)
    k, some = waiting[-1]
    projected_pair = project(gathered[k], some, projected, (q_cols, 2 * HEAD))
    projected_queries = project(gathered[k], some, projected, (0, q_cols))

    level_ids = jnp.arange(rows, dtype=jnp.int32)
    pair_ids = jnp.concatenate([my_inner * rows + level_ids, my_outer * rows + level_ids])
    row_ids = jnp.tile(pair_ids, n_f)
    digits = gathered[1][:, part:part + 2].astype(jnp.int32)
    starts = digits[:, 0] * 256 + digits[:, 1]
    cosine, sine = rotary_tables((row_ids - starts).astype(jnp.float32))

    key_rows = projected_pair[:, :HEAD]
    key_rows = key_rows + lax.dynamic_slice_in_dim(key_bias, kv_head * HEAD, HEAD)
    turned = jnp.concatenate([key_rows[:, HEAD // 2:], key_rows[:, :HEAD // 2]], axis=-1)
    keys = (key_rows * cosine + turned * sine).astype(jnp.bfloat16)
    values = projected_pair[:, HEAD:] + lax.dynamic_slice_in_dim(value_bias, kv_head * HEAD, HEAD)
    values = values.astype(jnp.bfloat16)
    pair_rows = 2 * rows
    key_value = jnp.concatenate(
        [keys.reshape(n_f, pair_rows, HEAD), values.reshape(n_f, pair_rows, HEAD)], axis=-1
    )
    start = None
    if groups:
        start = send(at_inner[0][:cut], shift(1))
        key_value, start = tie((key_value, start))
    seen = [key_value]
    reach = min(n_t - 1, -(-(LONGEST - 1) // rows))
    for s in range(1, min(n_pairs - 1, (reach + 1) // 2) + 1):
        seen.append(send(key_value, [(inner[j - s], inner[j]) for j in range(s, n_pairs)]))
    if groups:
        rest, projected_queries = tie((at_inner[0][cut:], projected_queries, seen[1]))[:2]
        got = send(rest, shift(1))
    if len(at_inner) < 2 * cuts:
        at_outer.append(outer_run(1))
        at_inner.append(send(at_outer[1], inward))

    def attend(outer_rows):
        blocks, columns = [], []
        for d in range(reach + 1):
            found = []
            for parity in range(2):
                offset = (1 - parity) ^ outer_rows
                s = -((offset - d) // 2)
                place = ((offset - d) % 2) ^ (1 - (parity + s) % 2)
                block = seen[s] if s < len(seen) else jnp.zeros_like(key_value)
                found.append(block[:, place * rows:(place + 1) * rows])
            blocks.append(jnp.where(pair % 2 == 0, found[0], found[1]))
            level = (my_outer if outer_rows else my_inner) - d
            columns.append(jnp.where(level >= 0, level * rows + level_ids, NOWHERE))
        return attention(
            outer_rows, rows=rows, groups=n_f, width=q_cols, f=f, projected=projected_queries,
            bias=lax.dynamic_slice_in_dim(query_bias, f * q_cols, q_cols)[None],
            cosine=cosine, sine=sine, starts=starts[:, None], row_ids=row_ids[:, None],
            columns=jnp.concatenate(columns)[None], key_value=jnp.concatenate(blocks, axis=1),
        )

    wide = lambda value: value.astype(jnp.float32)

    def multiply(item):
        if item[0] == 0:
            return partials_of_one(mixed, at_inner[item[1]], at_outer[item[1]], is_inner)
        return partials_of_two(mixed_inner, mixed_outer, arrived[item])

    def between_cores(items, long_ones):
        kept, given = [], []
        for item in items:
            if item == (0, 2 * cuts - 1) and kept:
                at_inner[-1], kept[-1] = tie((at_inner[-1], kept[-1]))
            a, b = multiply(item)
            kept, given = kept + [a], given + [b]
        given = tie((jnp.stack(given), long_ones))[0]
        return items, jnp.stack(kept), swap(given, 1, every)

    def between_chips(items, kept, given):
        crossed = []
        for d in range(2, n_f, 2):
            span = slice(d // 2 * rows, (d // 2 + 1) * rows)
            share = wide(kept[:, span]) + wide(given[:, span])
            crossed.append(swap(share.astype(jnp.bfloat16), d, every))
        return items, [kept, given] + crossed

    def between_levels(items, terms):
        others = [i for i, item in enumerate(items) if item[0]]
        if not others:
            return items, terms, None
        sums = [
            sum(wide(term[i, :rows, half * cut:]) for term in terms).astype(jnp.bfloat16)
            for i in others
        ]
        return items, terms, send(jnp.stack(sums), outward)

    def put_own(result, items, terms):
        for i, item in enumerate(items):
            if item[0] == 0:
                result = add_up(
                    result, hidden_in, terms, i, None, 0, is_inner, n_f,
                    order[1 - item[1] // cuts], n_t, cuts, cut, item[1] % cuts, 0)
        return result

    def put_others(result, items, terms, other):
        others = [i for i, item in enumerate(items) if item[0]]
        for n, i in enumerate(others):
            s, r, p = items[i]
            result = add_up(
                result, hidden_in, terms, i, other, n, is_inner, half,
                order[2 * s + 1 - r // cuts], n_t, cuts, cut, r % cuts, p * half)
        return result

    mixed_outer = attend(1)
    mixed_outer, at_inner, at_outer, projected_queries, seen, got = tie(
        (mixed_outer, at_inner, at_outer, projected_queries, seen, got))
    if groups:
        arrive(groups[0], jnp.concatenate([start, got], axis=0))
    runs = [(0, r) for r in range(2 * cuts)]
    result, phase, from_cores, from_chips, from_levels = hidden_in, 1, None, None, None
    while True:
        got = send_group(groups[phase]) if phase < len(groups) else None
        if len(at_inner) < 2 * cuts:
            at_outer.append(outer_run(len(at_inner)))
            at_inner.append(send(at_outer[-1], inward))
        received, crossed = from_levels, from_chips
        from_levels = between_levels(*from_chips) if from_chips else None
        from_chips = between_chips(*from_cores) if from_cores else None
        if phase == 1:
            there = send(mixed_outer, outward)
            mixed_inner = attend(0)
            mixed = jnp.where(is_inner, mixed_inner, there)
        items = list(groups[phase - 1]) if phase <= len(groups) else []
        ready = runs[:cuts]
        items, runs = items + ready, runs[cuts:]
        if phase >= len(groups) and not runs:
            break
        if received:
            result = put_others(result, *received)
        if crossed:
            result = put_own(result, *crossed)
        long_ones = (result, got, at_inner[-1:], from_chips and from_chips[1], from_levels and from_levels[2], there)
        from_cores = between_cores(items, long_ones) if items else None
        moving = [None if x is None else x[1:] for x in (from_cores, from_chips, from_levels)]
        moving, got, at_inner, at_outer, result = tie((moving, got, at_inner, at_outer, result))
        from_cores, from_chips, from_levels = [
            None if x is None else (x[0],) + tuple(y)
            for x, y in zip((from_cores, from_chips, from_levels), moving)
        ]
        if got is not None:
            arrive(groups[phase], got)
        phase += 1

    if received:
        result = put_others(result, *received)
    items, kept, given = between_cores(items, (from_chips and from_chips[1], result))
    final = between_chips(items, kept, given)
    if crossed:
        result = put_own(result, *crossed)
    if from_levels:
        result = put_others(result, *from_levels)
    before = between_levels(*from_chips) if from_chips else None
    terms, moved, result = tie((final[1], before and before[1:], result))
    if before:
        result = put_others(put_own(result, before[0], moved[0]), before[0], *moved)
    return put_others(put_own(result, items, terms), *between_levels(items, terms))


def solution(mesh):
    return jax.shard_map(
        per_device,
        mesh=mesh,
        in_specs=(
            P(("groups", "fsdp", "tp"), None),
            P(("groups", "fsdp", "tp")),
            P("groups"),
            P(("groups", "fsdp", "tp"), None),
            P(("groups", "fsdp", "tp"), None),
            P(("groups", "fsdp", "tp"), None),
            P(("groups", "fsdp", "tp"), None),
            P("groups"),
            P("groups"),
            P("groups"),
        ),
        out_specs=P(("groups", "fsdp", "tp"), None),
        check_vma=False,
    )
```

```python
import functools

import jax
import jax.numpy as jnp
from jax import lax
from jax.experimental import pallas as pl
from jax.experimental.pallas import tpu as pltpu
from jax.sharding import PartitionSpec as P

HEAD = 128
LONGEST = 512
rope_base = 1000000.0
norm_eps = 1e-06
MASKED = -1e30
LOG2E = 1.4426950408889634
NOWHERE = 1 << 20
LEVEL = ("fsdp", "tp")


LIGHT = pl.CostEstimate(flops=1, bytes_accessed=1, transcendentals=0)
ROOM = pltpu.CompilerParams(vmem_limit_bytes=48 << 20)


def normalize(hidden, gain, order, n_f, depth, cuts):
    rows, width = hidden.shape
    n_t, cut = len(order), depth // cuts
    places = [(k, h, i) for k in range(n_t) for h in range(cuts) for i in range(n_f)]

    def scale(hidden):
        widened = hidden.astype(jnp.float32)
        return lax.rsqrt(jnp.mean(widened * widened, axis=-1, keepdims=True) + norm_eps)

    if cut % 128:
        normed = (hidden.astype(jnp.float32) * scale(hidden) * gain).astype(jnp.bfloat16)
        return jnp.concatenate([
            lax.dynamic_slice_in_dim(normed, (i * n_t + order[k]) * depth + h * cut, cut, 1)
            for k, h, i in places
        ], axis=1)

    def kernel(order_ref, hidden_ref, gain_ref, out_ref):
        factor = scale(hidden_ref[...])
        for place, (k, h, i) in enumerate(places):
            start = pl.multiple_of((i * n_t + order_ref[k]) * depth + h * cut, cut)
            span = pl.ds(start, cut)
            run = hidden_ref[:, span].astype(jnp.float32) * factor * gain_ref[:, span]
            out_ref[:, place * cut:(place + 1) * cut] = run.astype(jnp.bfloat16)

    block = min(64, rows)
    own = pl.BlockSpec((block, width), lambda m, order_ref: (m, 0))
    return pl.pallas_call(
        kernel,
        grid_spec=pltpu.PrefetchScalarGridSpec(
            num_scalar_prefetch=1,
            grid=(rows // block,),
            in_specs=[own, pl.BlockSpec((1, width), lambda m, order_ref: (0, 0))],
            out_specs=own,
        ),
        out_shape=jax.ShapeDtypeStruct(hidden.shape, jnp.bfloat16),
        compiler_params=ROOM,
        cost_estimate=LIGHT,
    )(jnp.stack(order).astype(jnp.int32), hidden, gain[None])


def segment_starts(segments):
    places = jnp.arange(segments.shape[-1], dtype=jnp.int32)
    same = segments[:, None] == segments[None, :]
    return jnp.min(jnp.where(same, places, segments.shape[-1]), axis=-1)


def rotary_tables(positions):
    half = HEAD // 2
    frequency = rope_base ** (-(jnp.arange(half, dtype=jnp.float32) * 2.0 / HEAD))
    angles = positions[:, None] * frequency[None, :]
    cosine, sine = jnp.cos(angles), jnp.sin(angles)
    return jnp.concatenate([cosine, cosine], -1), jnp.concatenate([-sine, sine], -1)


def attention_kernel(heads, scale, n_keys, q_ref, bias_ref, cos_ref, sin_ref, start_ref, row_ref,
                     col_ref, k_ref, v_ref, out_ref):
    cosine, sine = cos_ref[...], sin_ref[...]
    columns = col_ref[:, :n_keys]
    allowed = (columns >= start_ref[...]) & (columns <= row_ref[...])
    keys, values = k_ref[0, :n_keys], v_ref[0, :n_keys]
    rows, together = out_ref.shape[0], min(4, heads)
    for first in range(0, heads, together):
        spans = [slice(h * HEAD, (h + 1) * HEAD) for h in range(first, first + together)]
        queries = []
        for span in spans:
            query = q_ref[:, span] + bias_ref[:, span]
            query = query * cosine + pltpu.roll(query, HEAD // 2, 1) * sine
            queries.append(query.astype(jnp.bfloat16))
        scores = lax.dot_general(
            jnp.concatenate(queries, axis=0), keys, (((1,), (1,)), ((), ())),
            preferred_element_type=jnp.float32,
        )
        probs = []
        for i in range(together):
            score = jnp.where(allowed, scores[i * rows:(i + 1) * rows], MASKED)
            highest = jnp.max(score, axis=-1, keepdims=True)
            weights = jnp.exp2((score - highest) * (scale * LOG2E))
            share = 1.0 / jnp.sum(weights, axis=-1, keepdims=True)
            probs.append((weights * share).astype(jnp.bfloat16))
        mixed = jnp.dot(
            jnp.concatenate(probs, axis=0), values, preferred_element_type=jnp.float32)
        for i, span in enumerate(spans):
            out_ref[:, span] = mixed[i * rows:(i + 1) * rows].astype(jnp.bfloat16)


def attention(part, *, rows, groups, width, f, projected, bias, cosine, sine, starts, row_ids,
              columns, key_value, near, limit):
    n_keys = key_value.shape[1]
    mine = lambda g, f_ref: (2 * g + part, 0)

    def place(g, f_ref):
        d = g ^ f_ref[0]
        return (d // 2 + (d % 2) * (groups // 2), 0)

    far = starts.reshape(groups, 2, rows)[:, part, 0] < limit

    def kernel(f_ref, *refs):
        is_far = f_ref[1 + pl.program_id(0)] == 1
        for taken, count in ((is_far, n_keys), (jnp.logical_not(is_far), near)):
            pl.when(taken)(functools.partial(
                attention_kernel, width // HEAD, HEAD ** -0.5, count, *refs))

    return pl.pallas_call(
        kernel,
        grid_spec=pltpu.PrefetchScalarGridSpec(
            num_scalar_prefetch=1,
            grid=(groups,),
            in_specs=[
                pl.BlockSpec((rows, width), mine),
                pl.BlockSpec((1, width), lambda g, f_ref: (0, 0)),
                pl.BlockSpec((rows, HEAD), mine),
                pl.BlockSpec((rows, HEAD), mine),
                pl.BlockSpec((rows, 1), mine),
                pl.BlockSpec((rows, 1), mine),
                pl.BlockSpec((1, n_keys), lambda g, f_ref: (0, 0)),
                pl.BlockSpec((1, n_keys, HEAD), lambda g, f_ref: (g, 0, 0)),
                pl.BlockSpec((1, n_keys, HEAD), lambda g, f_ref: (g, 0, 1)),
            ],
            out_specs=pl.BlockSpec((rows, width), place),
        ),
        out_shape=jax.ShapeDtypeStruct((groups * rows, width), jnp.bfloat16),
        compiler_params=ROOM,
        cost_estimate=LIGHT,
    )(jnp.concatenate([jnp.full((1,), f, jnp.int32), far.astype(jnp.int32)]), projected, bias, cosine, sine, starts, row_ids, columns,
      key_value, key_value)


def project(tokens, weights, total=None, columns=None):
    n_rows, width = tokens.shape[0], weights[0].shape[1]
    block, n_w = min(512, n_rows), len(weights)
    first, width = (0, width) if columns is None else columns
    at = first // width

    def kernel(*refs):
        part, done = None, 0
        for ref in refs[1:1 + n_w]:
            depth = ref.shape[0]
            more = jnp.dot(
                refs[0][:, done:done + depth], ref[...], preferred_element_type=jnp.float32
            )
            part, done = more if part is None else part + more, done + depth
        refs[-1][...] = part if total is None else part + refs[1 + n_w][...]

    sums = pl.BlockSpec((block, width), lambda m: (m, at))
    return pl.pallas_call(
        kernel,
        grid=(n_rows // block,),
        in_specs=[pl.BlockSpec((block, tokens.shape[1]), lambda m: (m, 0))]
        + [pl.BlockSpec((w.shape[0], width), lambda m: (0, at)) for w in weights]
        + ([] if total is None else [sums]),
        out_specs=pl.BlockSpec((block, width), lambda m: (m, 0)),
        out_shape=jax.ShapeDtypeStruct((n_rows, width), jnp.float32),
        input_output_aliases={1 + n_w: 0} if total is not None and columns is None else {},
        compiler_params=ROOM,
        cost_estimate=LIGHT,
    )(tokens, *weights, *([] if total is None else [total]))


def times_transposed(left, right):
    return lax.dot_general(
        left, right, (((1,), (1,)), ((), ())), preferred_element_type=jnp.float32
    ).astype(jnp.bfloat16)


def partials_of_one(mixed, first, second, take_first):
    n_rows, depth = mixed.shape
    width = first.shape[0]
    block = n_rows // 2

    def kernel(take_ref, mixed_ref, first_ref, second_ref, kept_ref, given_ref):
        def multiply(weight_ref, out_ref):
            out_ref[...] = times_transposed(mixed_ref[...], weight_ref[...])

        for taken, weight_ref in ((1, first_ref), (0, second_ref)):
            for half, out_ref in enumerate((given_ref, kept_ref)):
                chosen = (take_ref[0] == taken) & (pl.program_id(0) == half)
                pl.when(chosen)(functools.partial(multiply, weight_ref, out_ref))

    whole = lambda m, take_ref: (0, 0)
    return pl.pallas_call(
        kernel,
        grid_spec=pltpu.PrefetchScalarGridSpec(
            num_scalar_prefetch=1,
            grid=(2,),
            in_specs=[
                pl.BlockSpec((block, depth), lambda m, take_ref: (1 - m, 0)),
                pl.BlockSpec((width, depth), whole),
                pl.BlockSpec((width, depth), whole),
            ],
            out_specs=[pl.BlockSpec((block, width), whole)] * 2,
        ),
        out_shape=[jax.ShapeDtypeStruct((block, width), jnp.bfloat16)] * 2,
        compiler_params=ROOM,
        cost_estimate=LIGHT,
    )(jnp.full((1,), take_first, jnp.int32), mixed, first, second)


def partials_of_two(mixed_a, mixed_b, weight):
    n_rows, depth = mixed_a.shape
    width = weight.shape[0]
    block = n_rows // 2

    def kernel(a_ref, b_ref, weight_ref, kept_ref, given_ref):
        step = pl.program_id(0)
        for place, mixed_ref in enumerate((a_ref, b_ref)):
            for half, out_ref in enumerate((given_ref, kept_ref)):
                def multiply(mixed_ref=mixed_ref, out_ref=out_ref):
                    out_ref[...] = times_transposed(mixed_ref[...], weight_ref[...])

                pl.when(step == 2 * half + place)(multiply)

    rows = pl.BlockSpec((block, depth), lambda m: (1 - m // 2, 0))
    return pl.pallas_call(
        kernel,
        grid=(4,),
        in_specs=[rows, rows, pl.BlockSpec((width, depth), lambda m: (0, 0))],
        out_specs=[
            pl.BlockSpec((block, width), lambda m: (0, jnp.maximum(m - 2, 0))),
            pl.BlockSpec((block, width), lambda m: (0, jnp.minimum(m, 1))),
        ],
        out_shape=[jax.ShapeDtypeStruct((block, 2 * width), jnp.bfloat16)] * 2,
        compiler_params=ROOM,
        cost_estimate=LIGHT,
    )(mixed_a, mixed_b, weight)


def add_up(result, hidden, terms, item, other, other_item, use_terms, count, level, n_t, cuts, cut, h, first):
    rows = result.shape[0]
    wide = lambda term: term.astype(jnp.float32)
    if cut % 128:
        total = sum(wide(term[item, :rows, :count * cut]) for term in terms)
        if other is not None:
            total = jnp.where(use_terms, total, wide(other[other_item]))
        for i in range(count):
            column = ((first + i) * n_t + level) * cuts * cut + h * cut
            before = wide(lax.dynamic_slice_in_dim(hidden, column, cut, 1))
            result = lax.dynamic_update_slice_in_dim(
                result, (before + total[:, i * cut:(i + 1) * cut]).astype(jnp.bfloat16), column, 1)
        return result

    def kernel(at_ref, result_ref, hidden_ref, *refs):
        total = sum(wide(ref[...]) for ref in refs[:len(terms)])
        if other is not None:
            total = jnp.where(at_ref[1] == 1, total, wide(refs[len(terms)][...]))
        refs[-1][...] = (wide(hidden_ref[...]) + total).astype(jnp.bfloat16)

    place = pl.BlockSpec(
        (rows, cut), lambda i, at_ref: (0, ((first + i) * n_t + at_ref[0]) * cuts + h))
    one = lambda item: pl.BlockSpec((None, rows, cut), lambda i, at_ref: (item, 0, i))
    extra = [] if other is None else [other]
    return pl.pallas_call(
        kernel,
        grid_spec=pltpu.PrefetchScalarGridSpec(
            num_scalar_prefetch=1,
            grid=(count,),
            in_specs=[pl.BlockSpec(memory_space=pl.ANY), place]
            + [one(item)] * len(terms) + [one(other_item)] * len(extra),
            out_specs=place,
        ),
        out_shape=jax.ShapeDtypeStruct(result.shape, result.dtype),
        input_output_aliases={1: 0},
        compiler_params=ROOM,
        cost_estimate=LIGHT,
    )(jnp.stack([level, use_terms.astype(jnp.int32)]), result, hidden, *terms, *extra)


def per_device(
    hidden_in,
    segment_ids,
    norm_gain,
    query_weight,
    key_weight,
    value_weight,
    output_weight,
    query_bias,
    key_bias,
    value_bias,
):
    n_f, n_t = lax.axis_size("fsdp"), lax.axis_size("tp")
    f, t = lax.axis_index("fsdp"), lax.axis_index("tp")
    rows, width = hidden_in.shape
    depth = query_weight.shape[0]
    q_cols = query_weight.shape[1] // n_f
    kv_heads = key_weight.shape[1] // HEAD
    kv_head = f * kv_heads // n_f
    cuts = max(1, depth // 256)
    cut = depth // cuts
    n_pairs = n_t // 2
    inner = [2 * j + 1 - j % 2 for j in range(n_pairs)]
    outer = [2 * j + j % 2 for j in range(n_pairs)]
    pair = t // 2
    my_inner = 2 * pair + 1 - pair % 2
    my_outer = 2 * pair + pair % 2
    is_inner = t == my_inner
    inward = [(outer[j], inner[j]) for j in range(n_pairs)]
    outward = [(inner[j], outer[j]) for j in range(n_pairs)]
    every = list(range(n_t))
    tie = lax.optimization_barrier

    def shift(s):
        return [(inner[(j + s) % n_pairs], inner[j]) for j in range(n_pairs)]

    def send(value, pairs):
        return lax.ppermute(value, "tp", pairs)

    def swap(value, d, levels):
        return lax.ppermute(value, LEVEL, [
            (i * n_t + z, (i ^ d) * n_t + z) for i in range(n_f) for z in levels
        ])

    order = []
    for s in range(n_pairs):
        p = (pair + s) % n_pairs
        order += [2 * p + 1 - p % 2, 2 * p + p % 2]

    def by_index(pieces):
        bit = 1
        while bit < n_f:
            here = (f & bit) != 0
            pieces = [jnp.where(here, pieces[d ^ bit], pieces[d]) for d in range(n_f)]
            bit *= 2
        return jnp.concatenate(pieces, axis=0)

    def level_exchange(block_for, levels):
        return by_index([block_for(f)] + [
            swap(block_for(f ^ d), d, levels) for d in range(1, n_f)
        ])

    def projection_block(weights, h):
        def block(c):
            head = c * kv_heads // n_f
            span = slice(h * cut, (h + 1) * cut)
            return jnp.concatenate([
                lax.dynamic_slice_in_dim(weights[0][span], c * q_cols, q_cols, 1),
                lax.dynamic_slice_in_dim(weights[1][span], head * HEAD, HEAD, 1),
                lax.dynamic_slice_in_dim(weights[2][span], head * HEAD, HEAD, 1),
            ], axis=1)
        return block

    weights = (query_weight, key_weight, value_weight)
    mine = normalize(hidden_in, norm_gain, order, n_f, depth, cuts)
    part = n_f * depth

    def gather(k, theirs, outputs):
        both = jnp.concatenate([mine[:, k * part:(k + 1) * part], theirs], axis=0)
        chunks = outputs.shape[1] // part
        outputs = jnp.concatenate(
            [outputs[:, c * part:(c + 1) * part] for c in range(chunks)], axis=0)
        payload = jnp.where(is_inner, both, outputs)
        if k == 1:
            payload = jnp.concatenate(
                [payload, jnp.concatenate([digits, tail[:, width - early:]], axis=0)], axis=1)
        return lax.all_gather(payload, "fsdp", axis=0, tiled=True)

    def output_rows(gathered, count):
        blocks = gathered.reshape(n_f, -1, count, gathered.shape[1])
        column = f * q_cols
        blocks = lax.dynamic_slice(
            blocks, (0, column // part, 0, column % part), (n_f, 1, count, q_cols))
        return blocks.reshape(n_f, count, q_cols)

    count = 2 * rows * part // output_weight.shape[1]
    early = part

    own = [level_exchange(projection_block(weights, 0), every)]
    head = send(mine[:, :early], inward)
    own, weights, segment_ids = tie((own, weights, segment_ids))

    segments = lax.all_gather(segment_ids, "tp", axis=0, tiled=True)
    own, segments = tie((own, segments))
    my_starts = lax.dynamic_slice_in_dim(segment_starts(segments), t * rows, rows)
    digits = jnp.stack([my_starts // 256, my_starts % 256], axis=1).astype(jnp.bfloat16)
    digits = jnp.pad(digits, ((0, 0), (0, HEAD - 2)))
    tail = send(jnp.concatenate([mine[:, early:], digits], axis=1), inward)
    raw = []

    def source(k):
        runs = cut // count
        run, at = k // runs, (k % runs) * count
        if run >= 2 * cuts:
            return jnp.zeros((count, output_weight.shape[1]), output_weight.dtype)
        some = raw[run - cuts] if run >= cuts else output_weight[run * cut:(run + 1) * cut]
        return some[at:at + count]

    across = [send(own[0], shift(1))] if n_pairs > 1 else []
    own += [level_exchange(projection_block(weights, h), every) for h in range(1, cuts)]
    gathered = [gather(0, tie((head, own[0]))[0][:, :part], source(0))]
    own, across, tail, mine, output_weight = tie((own, across, tail, mine, output_weight))
    theirs = jnp.concatenate([head, tail[:, :width - early]], axis=1)

    beyond = []
    projected = None
    for h in range(cuts):
        until = min(n_t, (cuts + h) * (cut // count))
        gathered += [
            gather(k, theirs[:, k * part:(k + 1) * part], source(k))
            for k in range(len(gathered), until)
        ]
        if n_pairs > 1 and h + 1 < cuts:
            across.append(send(own[h + 1], shift(1)))
        elif n_pairs > 1 and h:
            across.append(send(beyond[0], shift(1)))
        beyond.append(send(own[h], inward))
        raw.append(send(output_weight[h * cut:(h + 1) * cut], outward))
        if h == 0:
            projected = project(gathered[0], own)
        own, beyond, across, raw, output_weight, projected, theirs, mine = tie(
            (own, beyond, across, raw, output_weight, projected, theirs, mine))
    gathered += [
        gather(k, theirs[:, k * part:(k + 1) * part], source(k)) for k in range(len(gathered), n_t)
    ]

    def outer_run(r):
        return jnp.concatenate([
            output_rows(gathered[k], count)
            for k in range(r * (cut // count), (r + 1) * (cut // count))
        ], axis=1).reshape(-1, q_cols)

    at_outer = [outer_run(0)]
    at_inner = [send(at_outer[0], inward)]
    if n_pairs > 1:
        across += [send(w, shift(1)) for w in beyond[len(across) - cuts:]]
    waiting = [(1, beyond)]
    if n_pairs > 1:
        projected = project(gathered[1], beyond, projected)
        projected = project(gathered[2], across[:cuts], projected)
        waiting = [(3, across[cuts:])]
    projected, across, at_inner, at_outer = tie((projected, across, at_inner, at_outer))

    groups = []
    half = n_f // 2
    for s in range(1, n_pairs):
        halves = [(s, r, p) for r in range(2 * cuts) for p in range(2)]
        groups += [halves[i:i + 2] for i in range(0, len(halves), 2)]

    def send_group(group):
        return send(jnp.concatenate([
            at_inner[r][p * half * cut:(p + 1) * half * cut] for _, r, p in group
        ], axis=0), shift(group[0][0]))

    arrived = {}

    def arrive(group, got):
        for place, (s, r, p) in enumerate(group):
            arrived[s, r, p] = got[place * half * cut:(place + 1) * half * cut]

    for s in range(2, n_pairs):
        across = [send(w, shift(s)) for w in own + beyond]
        waiting += [(2 * s, across[:cuts]), (2 * s + 1, across[cuts:])]
    for k, some in waiting[:-1]:
        projected = project(gathered[k], some, projected)
    k, some = waiting[-1]
    projected_pair = project(gathered[k], some, projected, (q_cols, 2 * HEAD))
    projected_queries = project(gathered[k], some, projected, (0, q_cols))

    level_ids = jnp.arange(rows, dtype=jnp.int32)
    pair_ids = jnp.concatenate([my_inner * rows + level_ids, my_outer * rows + level_ids])
    row_ids = jnp.tile(pair_ids, n_f)
    digits = gathered[1][:, part:part + 2].astype(jnp.int32)
    starts = digits[:, 0] * 256 + digits[:, 1]
    cosine, sine = rotary_tables((row_ids - starts).astype(jnp.float32))

    key_rows = projected_pair[:, :HEAD]
    key_rows = key_rows + lax.dynamic_slice_in_dim(key_bias, kv_head * HEAD, HEAD)
    turned = jnp.concatenate([key_rows[:, HEAD // 2:], key_rows[:, :HEAD // 2]], axis=-1)
    keys = (key_rows * cosine + turned * sine).astype(jnp.bfloat16)
    values = projected_pair[:, HEAD:] + lax.dynamic_slice_in_dim(value_bias, kv_head * HEAD, HEAD)
    values = values.astype(jnp.bfloat16)
    pair_rows = 2 * rows
    key_value = jnp.concatenate(
        [keys.reshape(n_f, pair_rows, HEAD), values.reshape(n_f, pair_rows, HEAD)], axis=-1
    )
    start = None
    if groups:
        start = send(at_inner[0][:cut], shift(1))
        key_value, start = tie((key_value, start))
    seen = [key_value]
    reach = min(n_t - 1, -(-(LONGEST - 1) // rows))
    for s in range(1, min(n_pairs - 1, (reach + 1) // 2) + 1):
        seen.append(send(key_value, [(inner[j - s], inner[j]) for j in range(s, n_pairs)]))
    if groups:
        rest, projected_queries = tie((at_inner[0][cut:], projected_queries, seen[1]))[:2]
        got = send(rest, shift(1))
    if len(at_inner) < 2 * cuts:
        at_outer.append(outer_run(1))
        at_inner.append(send(at_outer[1], inward))

    def attend(outer_rows):
        blocks, columns = [], []
        for d in range(reach + 1):
            found = []
            for parity in range(2):
                offset = (1 - parity) ^ outer_rows
                s = -((offset - d) // 2)
                place = ((offset - d) % 2) ^ (1 - (parity + s) % 2)
                block = seen[s] if s < len(seen) else jnp.zeros_like(key_value)
                found.append(block[:, place * rows:(place + 1) * rows])
            blocks.append(jnp.where(pair % 2 == 0, found[0], found[1]))
            level = (my_outer if outer_rows else my_inner) - d
            columns.append(jnp.where(level >= 0, level * rows + level_ids, NOWHERE))
        return attention(
            outer_rows, rows=rows, groups=n_f, width=q_cols, f=f, projected=projected_queries,
            bias=lax.dynamic_slice_in_dim(query_bias, f * q_cols, q_cols)[None],
            cosine=cosine, sine=sine, starts=starts[:, None], row_ids=row_ids[:, None],
            columns=jnp.concatenate(columns)[None], key_value=jnp.concatenate(blocks, axis=1),
            near=reach * rows,
            limit=((my_outer if outer_rows else my_inner) - reach + 1) * rows,
        )

    wide = lambda value: value.astype(jnp.float32)

    def multiply(item):
        if item[0] == 0:
            return partials_of_one(mixed, at_inner[item[1]], at_outer[item[1]], is_inner)
        return partials_of_two(mixed_inner, mixed_outer, arrived[item])

    def between_cores(items, long_ones):
        kept, given = [], []
        for item in items:
            if item == (0, 2 * cuts - 1) and kept:
                at_inner[-1], kept[-1] = tie((at_inner[-1], kept[-1]))
            a, b = multiply(item)
            kept, given = kept + [a], given + [b]
        given = tie((jnp.stack(given), long_ones))[0]
        return items, jnp.stack(kept), swap(given, 1, every)

    def between_chips(items, kept, given):
        crossed = []
        for d in range(2, n_f, 2):
            span = slice(d // 2 * rows, (d // 2 + 1) * rows)
            share = wide(kept[:, span]) + wide(given[:, span])
            crossed.append(swap(share.astype(jnp.bfloat16), d, every))
        return items, [kept, given] + crossed

    def between_levels(items, terms):
        others = [i for i, item in enumerate(items) if item[0]]
        if not others:
            return items, terms, None
        sums = [
            sum(wide(term[i, :rows, half * cut:]) for term in terms).astype(jnp.bfloat16)
            for i in others
        ]
        return items, terms, send(jnp.stack(sums), outward)

    def put_own(result, items, terms):
        for i, item in enumerate(items):
            if item[0] == 0:
                result = add_up(
                    result, hidden_in, terms, i, None, 0, is_inner, n_f,
                    order[1 - item[1] // cuts], n_t, cuts, cut, item[1] % cuts, 0)
        return result

    def put_others(result, items, terms, other):
        others = [i for i, item in enumerate(items) if item[0]]
        for n, i in enumerate(others):
            s, r, p = items[i]
            result = add_up(
                result, hidden_in, terms, i, other, n, is_inner, half,
                order[2 * s + 1 - r // cuts], n_t, cuts, cut, r % cuts, p * half)
        return result

    mixed_outer = attend(1)
    mixed_outer, at_inner, at_outer, projected_queries, seen, got = tie(
        (mixed_outer, at_inner, at_outer, projected_queries, seen, got))
    if groups:
        arrive(groups[0], jnp.concatenate([start, got], axis=0))
    runs = [(0, r) for r in range(2 * cuts)]
    result, phase, from_cores, from_chips, from_levels = hidden_in, 1, None, None, None
    while True:
        got = send_group(groups[phase]) if phase < len(groups) else None
        if len(at_inner) < 2 * cuts:
            at_outer.append(outer_run(len(at_inner)))
            at_inner.append(send(at_outer[-1], inward))
        received, crossed = from_levels, from_chips
        from_levels = between_levels(*from_chips) if from_chips else None
        from_chips = between_chips(*from_cores) if from_cores else None
        if phase == 1:
            there = send(mixed_outer, outward)
            mixed_inner = attend(0)
            mixed = jnp.where(is_inner, mixed_inner, there)
        items = list(groups[phase - 1]) if phase <= len(groups) else []
        ready = runs[:cuts]
        items, runs = items + ready, runs[cuts:]
        if phase >= len(groups) and not runs:
            break
        if received:
            result = put_others(result, *received)
        if crossed:
            result = put_own(result, *crossed)
        long_ones = (result, got, at_inner[-1:], from_chips and from_chips[1], from_levels and from_levels[2], there)
        from_cores = between_cores(items, long_ones) if items else None
        moving = [None if x is None else x[1:] for x in (from_cores, from_chips, from_levels)]
        moving, got, at_inner, at_outer, result = tie((moving, got, at_inner, at_outer, result))
        from_cores, from_chips, from_levels = [
            None if x is None else (x[0],) + tuple(y)
            for x, y in zip((from_cores, from_chips, from_levels), moving)
        ]
        if got is not None:
            arrive(groups[phase], got)
        phase += 1

    if received:
        result = put_others(result, *received)
    items, kept, given = between_cores(items, (from_chips and from_chips[1], result))
    final = between_chips(items, kept, given)
    if crossed:
        result = put_own(result, *crossed)
    if from_levels:
        result = put_others(result, *from_levels)
    before = between_levels(*from_chips) if from_chips else None
    terms, moved, result = tie((final[1], before and before[1:], result))
    if before:
        result = put_others(put_own(result, before[0], moved[0]), before[0], *moved)
    return put_others(put_own(result, items, terms), *between_levels(items, terms))


def solution(mesh):
    return jax.shard_map(
        per_device,
        mesh=mesh,
        in_specs=(
            P(("groups", "fsdp", "tp"), None),
            P(("groups", "fsdp", "tp")),
            P("groups"),
            P(("groups", "fsdp", "tp"), None),
            P(("groups", "fsdp", "tp"), None),
            P(("groups", "fsdp", "tp"), None),
            P(("groups", "fsdp", "tp"), None),
            P("groups"),
            P("groups"),
            P("groups"),
        ),
        out_specs=P(("groups", "fsdp", "tp"), None),
        check_vma=False,
    )
```
